32 devices in a mesh: rep: 2 (over x), dp: 2 (over core), tensor: 8 (over z, y).
Axes of the slice: x: 2, y: 2, z: 4, core: 2. Of those that a mesh axis runs over, the one named last changes fastest.
Arguments:
- hidden: bfloat16 [1024, 8192], P(('rep', 'dp'), 'tensor'), parts along dimension 0, may hold values from -6 to 6
- attn_gain: float32 [8192], replicated, may hold values from 0.25 to 1.75
- q_weight: bfloat16 [8192, 2048], P('dp', 'tensor'), may hold values from -0.0625 to 0.0625
- kv_weight: bfloat16 [8192, 256], P('tensor'), may hold values from -0.0625 to 0.0625
- kv_cache: bfloat16 [16, 256, 256], P(('rep', 'dp')), parts along dimension 0, may hold values from -200 to 200
- out_weight: bfloat16 [2048, 8192], P('tensor', 'dp'), may hold values from -0.5 to 0.5
- final_gain: float32 [8192], replicated, may hold values from 0.25 to 1.75
- vocab_weight: bfloat16 [8192, 4096], P('dp', 'tensor'), may hold values from -80 to 80
- resp_len: int32 [16], P('rep'), parts along dimension 0, may hold values from 1 to 128, as said below
- ctx_len: int32 [16], P(('rep', 'dp')), parts along dimension 0, may hold values from 1 to 256
- target_ids: int32 [1024], P('rep'), parts along dimension 0, may hold values from 0 to 4095
Outputs:
- layer_out: bfloat16 [1024, 8192], P(('rep', 'dp'), 'tensor'), parts along dimension 0
- token_logprob: float32 [1024], P(('rep', 'dp')), parts along dimension 0
The draws below stay inside these ranges and needn't reach their ends.
There are 2 independent parts, one for each index of `rep`. The reference program is written for one: setup_inputs(seed, part) draws one part's arguments, and reference() takes and returns one part's arrays. A program takes and returns all parts, laid end to end along the dimension named above; an argument that names none is the same for every part. Nothing has to cross between parts.
Inputs may be any that keep to these rules, and one draw needn't show every extreme that they name: `resp_len`: within a data group the rollouts fill its first slots in order. The lengths of the two data groups of a part add up to exactly 256, so one group has more than 128 live slots and the other fewer; one rollout of the busier group has exactly 128 slots.
All inputs are finite; a program needn't handle non-finite values.
Results may differ from the reference program's by a relative error of at most 0.015.
The reference program's roundings to bfloat16 on the way (of `normed`, `query`, `keyval`, `probs`, `attn` and `final`) count: a program that leaves them out, or rounds other values in their place, can miss the bound.
Values may be sent and summed in bfloat16 or wider, within the bound.
No kernel may reach another device: no remote copies, remote signals or barrier semaphores. Data moves between devices by JAX's collectives and lax.ppermute only.
A program may use at most 128 MiB of HBM per device.

```python
import jax
import jax.numpy as jnp
from jax import lax

D = 8192
HEAD = 128
QH_DEV = 2
GROUP = 16
ROWS = 256
SEQS = 4
CTX = 256
QHEADS = 16
KVH = 1
VOCAB = 4096
N_DP = 2
N_TENSOR = 8


def split_total(total, weights):
    count = weights.shape[0]
    spare = total - count
    shares = 1 + weights * spare // jnp.sum(weights)
    return shares.at[count - 1].add(total - jnp.sum(shares))


def draw_resp_len(key, part):
    key = jax.random.fold_in(key, 11)
    first, second, third, fourth = jax.random.split(key, 4)
    half = ROWS // 2
    extra = jax.random.randint(first, (), SEQS, half - SEQS + 1)
    heavy_group = jax.random.randint(second, (), 0, 2)
    weights = jax.random.randint(third, (2, SEQS), 1, 9)
    place = jax.random.randint(fourth, (), 0, SEQS)
    rest = split_total(extra, weights[0, :SEQS - 1])
    index = jnp.arange(SEQS, dtype=jnp.int32)
    pick = jnp.clip(index - (index > place).astype(jnp.int32), 0, SEQS - 2)
    heavy = jnp.where(index == place, half, rest[pick])
    light = split_total(half - extra, weights[1])
    lengths = jnp.where(heavy_group == 0, jnp.concatenate([heavy, light]), jnp.concatenate([light, heavy]))
    return lengths.astype(jnp.int32)


def draw_kv_cache(key, part):
    key = jax.random.fold_in(key, 5)
    shape = (N_DP * SEQS, CTX, KVH * 2 * HEAD)
    values = jnp.clip(jax.random.normal(key, shape, jnp.float32), -5.0, 5.0)
    return values.astype(jnp.bfloat16)


def draw_vocab_weight(key, part):
    key = jax.random.fold_in(key, 7)
    base_key = jax.random.fold_in(key, 0)
    values = jnp.clip(jax.random.normal(base_key, (D, VOCAB), jnp.float32), -6.0, 6.0) * (D // 9) ** (-0.5)
    return values.astype(jnp.bfloat16)


def place_ends(values, key, low, high):
    index_at = [jax.random.randint(jax.random.fold_in(key, axis), (), 0, length) for axis, length in enumerate(values.shape)]
    main_axis = values.shape.index(max(values.shape))
    beside = index_at[:main_axis] + [(index_at[main_axis] + 1) % values.shape[main_axis]] + index_at[main_axis + 1:]
    return values.at[tuple(index_at)].set(low).at[tuple(beside)].set(high)


def levels(key, extent, cuts, least, top_value):
    def one(position, blocks):
        draws = jax.random.uniform(jax.random.fold_in(jax.random.fold_in(key, 6), position), (blocks,), jnp.float32, least / len(cuts), top_value / len(cuts))
        return jnp.repeat(jnp.exp(draws), extent[position] // blocks).reshape((-1,) + (1,) * (len(extent) - position - 1))

    level = one(*cuts[0])
    for cut in cuts[1:]:
        level = level * one(*cut)
    return level


def bell_draw(stream_key, extent, deviation, limit, pieces=(), kind=jnp.bfloat16):
    entries = jax.random.normal(stream_key, extent, jnp.float32) * deviation
    if len(pieces) > 0:
        entries = levels(stream_key, extent, pieces, -0.22, 0.18) * entries
    return jnp.clip(entries, min=-limit, max=limit).astype(kind)


def setup_inputs(seed: int = 0, part: int = 0) -> dict:
    arg_keys = jax.random.split(jax.random.key(seed), 12)
    own_keys = jax.random.split(jax.random.fold_in(arg_keys[11], part), 12)
    return {
        "hidden": bell_draw(own_keys[0], (N_DP * ROWS, D), 1.0, 6.0, ((0, 2), (1, 8))),
        "attn_gain": jnp.clip(1.0 + 0.15 * jax.random.normal(arg_keys[1], (D,), jnp.float32), 0.25, 1.75),
        "q_weight": bell_draw(arg_keys[2], (D, QHEADS * HEAD), D ** -0.5, 0.0625, ((0, 2), (1, 8))),
        "kv_weight": bell_draw(arg_keys[3], (D, KVH * 2 * HEAD), D ** -0.5, 0.0625, ((0, 8),)),
        "kv_cache": draw_kv_cache(jax.random.fold_in(jax.random.fold_in(arg_keys[11], part), 71), part),
        "out_weight": bell_draw(arg_keys[5], (QHEADS * HEAD, D), (QHEADS * HEAD // 16) ** -0.5, 0.5, ((0, 8), (1, 2))),
        "final_gain": jnp.clip(1.0 + 0.15 * jax.random.normal(arg_keys[6], (D,), jnp.float32), 0.25, 1.75),
        "vocab_weight": draw_vocab_weight(jax.random.fold_in(arg_keys[11], 71), part),
        "resp_len": draw_resp_len(jax.random.fold_in(jax.random.fold_in(arg_keys[11], part), 71), part),
        "ctx_len": place_ends(jax.random.randint(own_keys[9], (N_DP * SEQS,), 1, CTX + 1), jax.random.fold_in(own_keys[9], 1), 1, CTX).astype(jnp.int32),
        "target_ids": place_ends(jax.random.randint(own_keys[10], (N_DP * ROWS,), 0, VOCAB), jax.random.fold_in(own_keys[10], 1), 0, VOCAB - 1).astype(jnp.int32),
    }


EPS = 1e-05

def rms_scale(values):
    return lax.rsqrt(lax.optimization_barrier(jnp.mean(values * values, axis=-1, keepdims=True)) + EPS)

def one_group(rows_in, attn_gain, q_weight, kv_weight, cache, out_weight, final_gain, vocab_weight, lens, ctx, targets):
    width = QH_DEV * HEAD
    heads = QH_DEV * N_TENSOR
    rows_f = rows_in.astype(jnp.float32)
    normed = (rows_f * rms_scale(rows_f) * attn_gain).astype(jnp.bfloat16)
    query = jnp.dot(normed, q_weight, preferred_element_type=jnp.float32).astype(jnp.bfloat16).reshape(ROWS, heads, HEAD)
    keyval = jnp.dot(normed, kv_weight, preferred_element_type=jnp.float32).astype(jnp.bfloat16).reshape(ROWS, KVH, 2, HEAD)
    ends = jnp.cumsum(lens).astype(jnp.int32)
    row_ids = jnp.arange(ROWS, dtype=jnp.int32)
    seg = lax.optimization_barrier(jnp.sum((row_ids[:, None] >= ends[None, :]).astype(jnp.int32), axis=1))
    cache_flat = cache.reshape(SEQS * CTX, KVH, 2, HEAD)
    keys = jnp.concatenate([cache_flat[:, :, 0], keyval[:, :, 0]], axis=0)
    vals = jnp.concatenate([cache_flat[:, :, 1], keyval[:, :, 1]], axis=0)
    slot_seg = jnp.repeat(jnp.arange(SEQS, dtype=jnp.int32), CTX)
    slot_pos = jnp.tile(jnp.arange(CTX, dtype=jnp.int32), SEQS)
    ctx_ok = (slot_seg[None, :] == seg[:, None]) & (slot_pos < ctx[slot_seg])[None, :]
    own_ok = (seg[None, :] == seg[:, None]) & (row_ids[None, :] <= row_ids[:, None])
    allowed = jnp.concatenate([ctx_ok, own_ok], axis=1)
    kv_map = jnp.arange(heads, dtype=jnp.int32) // GROUP
    keys_h = keys[:, kv_map].astype(jnp.float32)
    vals_h = vals[:, kv_map].astype(jnp.float32)
    scores = jnp.einsum('rhe,khe->hrk', query.astype(jnp.float32), keys_h) * HEAD ** (-0.5)
    scores = jnp.where(allowed[None], scores, -jnp.inf)
    top = lax.optimization_barrier(jnp.max(scores, axis=2, keepdims=True))
    weights = jnp.exp(scores - top)
    probs = (weights / lax.optimization_barrier(jnp.sum(weights, axis=2, keepdims=True))).astype(jnp.bfloat16)
    attn = jnp.einsum('hrk,khe->rhe', probs.astype(jnp.float32), vals_h).astype(jnp.bfloat16).reshape(ROWS, heads * HEAD)

    def add_shard(total, index):
        left = lax.dynamic_slice_in_dim(attn, index * width, width, 1)
        right = lax.dynamic_slice_in_dim(out_weight, index * width, width, 0)
        product = jnp.dot(left, right, preferred_element_type=jnp.float32)
        return (total + lax.optimization_barrier(product.astype(jnp.bfloat16)).astype(jnp.float32), None)
    branch, _ = lax.scan(add_shard, jnp.zeros((ROWS, D), jnp.float32), jnp.arange(N_TENSOR, dtype=jnp.int32))
    mixed = rows_f + branch
    live = row_ids < ends[SEQS - 1]
    layer = jnp.where(live[:, None], mixed, 0.0).astype(jnp.bfloat16)
    final = (mixed * rms_scale(mixed) * final_gain).astype(jnp.bfloat16)
    logits = jnp.dot(final, vocab_weight, preferred_element_type=jnp.float32)
    top_logit = lax.optimization_barrier(jnp.max(logits, axis=1))
    total = lax.optimization_barrier(jnp.sum(jnp.exp(logits - top_logit[:, None]), axis=1))
    vocab_ids = jnp.arange(VOCAB, dtype=jnp.int32)
    picked = lax.optimization_barrier(jnp.sum(jnp.where(vocab_ids[None, :] == targets[:, None], logits, 0.0), axis=1))
    logprob = jnp.where(live, picked - top_logit - jnp.log(total), 0.0)
    return (layer, logprob)

def reference(hidden, attn_gain, q_weight, kv_weight, kv_cache, out_weight, final_gain, vocab_weight, resp_len, ctx_len, target_ids):
    layers = []
    logprobs = []
    for group in range(N_DP):
        layer, logprob = one_group(hidden[group * ROWS:(group + 1) * ROWS], attn_gain, q_weight, kv_weight, kv_cache[group * SEQS:(group + 1) * SEQS], out_weight, final_gain, vocab_weight, resp_len[group * SEQS:(group + 1) * SEQS], ctx_len[group * SEQS:(group + 1) * SEQS], target_ids[group * ROWS:(group + 1) * ROWS])
        layers.append(layer)
        logprobs.append(logprob)
    return (jnp.concatenate(layers, axis=0), jnp.concatenate(logprobs, axis=0))
```

```python
import jax
import jax.numpy as jnp
from jax import lax
from jax.sharding import PartitionSpec as P

HEAD = 128
QH_DEV = 2
GROUP = 16
SIDE = 2


EPS = 1e-05


def product(left, right):
    return jnp.dot(left, right, preferred_element_type=jnp.float32)


def swap_dp(value):
    return lax.ppermute(value, "dp", [(0, 1), (1, 0)])


def swap_side(value):
    count = lax.axis_size("tensor")
    return lax.ppermute(value, "tensor", [(i, i ^ 1) for i in range(count)])


def ring_step(value):
    count = lax.axis_size("tensor")
    return lax.ppermute(value, "tensor", [(i, (i + SIDE) % count) for i in range(count)])


def doubling(value, combine):
    count = lax.axis_size("tensor")
    step = 1
    while step < count:
        other = lax.ppermute(value, "tensor", [(i, i ^ step) for i in range(count)])
        value = combine(value, other, step)
        step *= 2
    return value


def sum_tensor(value):
    return doubling(value, lambda a, b, step: a + b)


def gather_blocks(block):
    blocks = []
    for k in range(lax.axis_size("tensor") // SIDE):
        if k > 0:
            block = ring_step(block)
        blocks.append(block)
        blocks.append(swap_side(block))
    return blocks


def gathered_ids():
    count = lax.axis_size("tensor")
    pos = lax.axis_index("tensor")
    ids = []
    for k in range(count // SIDE):
        held = (pos - SIDE * k + count) % count
        ids += [held, held ^ 1]
    return ids


def scattered_ids():
    count = lax.axis_size("tensor")
    pos = lax.axis_index("tensor")
    ids = []
    for k in range(count // SIDE):
        held = (pos - SIDE * (k + 1) + count) % count
        ids += [held, held ^ 1]
    return ids


def pick_blocks(own, other, ids, axis):
    count = lax.axis_size("tensor")
    size = own.shape[axis] * 2 // count
    group = lax.axis_index("dp")
    picked = []
    for block in ids:
        place = (block % (count // 2)) * size
        here = lax.dynamic_slice_in_dim(own, place, size, axis)
        there = lax.dynamic_slice_in_dim(other, place, size, axis)
        picked.append(jnp.where(block // (count // 2) == group, here, there))
    return picked


def row_segment(rows, lens):
    ends = jnp.cumsum(lens)
    return jnp.sum((rows[:, None] >= ends[None, :]).astype(jnp.int32), axis=1)


def per_device(
    hidden,
    attn_gain,
    q_weight,
    kv_weight,
    kv_cache,
    out_weight,
    final_gain,
    vocab_weight,
    resp_len,
    ctx_len,
    target_ids,
):
    rows_count, shard = hidden.shape
    half = rows_count // 2
    tensor_count = lax.axis_size("tensor")
    tensor_pos = lax.axis_index("tensor")
    group = lax.axis_index("dp")
    full_width = shard * tensor_count
    seqs_count, ctx_slots = kv_cache.shape[:2]

    own_lens = lax.dynamic_slice_in_dim(resp_len, group * seqs_count, seqs_count, 0)
    other_lens = lax.dynamic_slice_in_dim(resp_len, (1 - group) * seqs_count, seqs_count, 0)
    busy = jnp.sum(own_lens) > half
    busy_lens = jnp.where(busy, own_lens, other_lens)
    light_total = jnp.sum(jnp.where(busy, other_lens, own_lens))
    is_long = busy_lens == half
    long_seq = jnp.sum(jnp.where(is_long, jnp.arange(seqs_count, dtype=jnp.int32), 0))
    long_start = jnp.sum(jnp.where(is_long, jnp.cumsum(busy_lens) - busy_lens, 0))
    slot = jnp.arange(half, dtype=jnp.int32)
    rest = slot - light_total
    rest_row = rest + jnp.where(rest >= long_start, half, 0)
    keep_src = jnp.where(busy, long_start + slot, jnp.where(rest < 0, slot, -1))
    send_src = jnp.where(busy & (rest >= 0), rest_row, -1)
    row_ids = jnp.arange(rows_count, dtype=jnp.int32)
    keep_pick = keep_src[:, None] == row_ids[None, :]
    send_pick = send_src[:, None] == row_ids[None, :]
    pick = jnp.concatenate([keep_pick, send_pick], axis=0).astype(jnp.bfloat16)
    moved = product(pick, hidden).astype(jnp.bfloat16)
    rows = moved[:half] + swap_dp(moved[half:])

    own_seg = row_segment(slot, own_lens)
    rest_seg = seqs_count + row_segment(rest_row, busy_lens)
    seg = jnp.where(busy, long_seq, jnp.where(rest < 0, own_seg, rest_seg))
    target_row = jnp.where(
        busy,
        group * rows_count + long_start + slot,
        jnp.where(rest < 0, group * rows_count + slot, (1 - group) * rows_count + rest_row),
    )
    all_rows = jnp.arange(target_ids.shape[0], dtype=jnp.int32)
    targets = jnp.sum(jnp.where(target_row[:, None] == all_rows[None, :], target_ids[None, :], 0), axis=1)

    q_blocks = pick_blocks(q_weight, swap_dp(q_weight), gathered_ids(), 0)
    out_blocks = pick_blocks(out_weight, swap_dp(out_weight), scattered_ids(), 1)
    vocab_blocks = pick_blocks(vocab_weight, swap_dp(vocab_weight), gathered_ids(), 0)

    rows_f = rows.astype(jnp.float32)
    square_sum = sum_tensor(jnp.sum(rows_f * rows_f, axis=1)[None, :])[0]
    scale = lax.rsqrt(square_sum / full_width + EPS)[:, None]

    def normed_block(block, index):
        gain = lax.dynamic_slice_in_dim(attn_gain, index * shard, shard, 0)
        return (block.astype(jnp.float32) * scale * gain).astype(jnp.bfloat16)

    kv_head = tensor_pos * QH_DEV // GROUP
    kv_partial = product(normed_block(rows, tensor_pos), kv_weight)
    kv_all = sum_tensor(kv_partial).astype(jnp.bfloat16)
    new_kv = lax.dynamic_slice_in_dim(kv_all, kv_head * 2 * HEAD, 2 * HEAD, 1)
    cache = lax.dynamic_slice_in_dim(kv_cache, kv_head * 2 * HEAD, 2 * HEAD, 2).reshape(-1, 2 * HEAD)
    both_cache = jnp.concatenate([cache, swap_dp(cache)], axis=0)
    both_ctx = jnp.concatenate([ctx_len, swap_dp(ctx_len)], axis=0)
    keys = jnp.concatenate([both_cache[:, :HEAD], new_kv[:, :HEAD]], axis=0)
    vals = jnp.concatenate([both_cache[:, HEAD:], new_kv[:, HEAD:]], axis=0)
    both_seqs = 2 * seqs_count
    slot_seg = lax.broadcasted_iota(jnp.int32, (both_seqs, ctx_slots), 0).reshape(-1)
    slot_pos = lax.broadcasted_iota(jnp.int32, (both_seqs, ctx_slots), 1).reshape(-1)
    slot_len = jnp.broadcast_to(both_ctx[:, None], (both_seqs, ctx_slots)).reshape(-1)
    ctx_ok = (slot_seg[None, :] == seg[:, None]) & (slot_pos < slot_len)[None, :]
    own_ok = (seg[None, :] == seg[:, None]) & (slot[None, :] <= slot[:, None])
    allowed = jnp.concatenate([ctx_ok, own_ok], axis=1)

    query = 0.0
    for block, index, weight in zip(gather_blocks(rows), gathered_ids(), q_blocks):
        query = query + product(normed_block(block, index), weight)
    query = query.astype(jnp.bfloat16).reshape(half, QH_DEV, HEAD)
    scores = jnp.einsum("rhe,ke->hrk", query, keys, preferred_element_type=jnp.float32) * HEAD ** (
        -0.5
    )
    scores = jnp.where(allowed[None], scores, -jnp.inf)
    top = jnp.max(scores, axis=2, keepdims=True)
    weights = jnp.exp(scores - top)
    probs = (weights / jnp.sum(weights, axis=2, keepdims=True)).astype(jnp.bfloat16)
    attn = jnp.einsum("hrk,ke->rhe", probs, vals, preferred_element_type=jnp.float32)
    attn = attn.astype(jnp.bfloat16).reshape(half, QH_DEV * HEAD)

    partial = None
    for k in range(tensor_count // SIDE):
        mine = product(attn, out_blocks[2 * k]).astype(jnp.bfloat16).astype(jnp.float32)
        theirs = product(attn, out_blocks[2 * k + 1]).astype(jnp.bfloat16)
        total = mine + swap_side(theirs).astype(jnp.float32)
        if partial is not None:
            total = total + ring_step(partial).astype(jnp.float32)
        partial = total.astype(jnp.bfloat16)
    mixed = rows_f + total

    square_sum = sum_tensor(jnp.sum(mixed * mixed, axis=1)[None, :])[0]
    scale = lax.rsqrt(square_sum / full_width + EPS)[:, None]
    gain = lax.dynamic_slice_in_dim(final_gain, tensor_pos * shard, shard, 0)
    final_rows = (mixed * scale * gain).astype(jnp.bfloat16)
    logits = 0.0
    for block, weight in zip(gather_blocks(final_rows), vocab_blocks):
        logits = logits + product(block, weight)
    vocab_count = vocab_weight.shape[1]
    column_ids = tensor_pos * vocab_count + lax.broadcasted_iota(jnp.int32, (half, vocab_count), 1)
    picked = jnp.sum(jnp.where(column_ids == targets[:, None], logits, 0.0), axis=1)
    top = jnp.max(logits, axis=1)
    total = jnp.sum(jnp.exp(logits - top[:, None]), axis=1)

    def join(a, b, step):
        first = (tensor_pos // step) % 2 == 0
        a, b = jnp.where(first, a, b), jnp.where(first, b, a)
        top = jnp.maximum(a[0], b[0])
        total = a[1] * jnp.exp(a[0] - top) + b[1] * jnp.exp(b[0] - top)
        return jnp.stack([top, total, a[2] + b[2]])

    top, total, picked = doubling(jnp.stack([top, total, picked]), join)
    logprob = (picked - top - jnp.log(total))[None, :]

    layer_rows = mixed.astype(jnp.bfloat16)
    layer_rows = jnp.concatenate([layer_rows, swap_dp(layer_rows)], axis=0)
    layer_out = lax.dot_general(
        pick, layer_rows, (((0,), (0,)), ((), ())), preferred_element_type=jnp.float32
    ).astype(jnp.bfloat16)
    both_logprob = jnp.concatenate([logprob, swap_dp(logprob)], axis=1)
    both_pick = jnp.concatenate([keep_pick, send_pick], axis=0)
    token_logprob = jnp.sum(jnp.where(both_pick, both_logprob.reshape(-1, 1), 0.0), axis=0)
    return (layer_out, token_logprob)


def solution(mesh):
    placed = (
        P(("rep", "dp"), "tensor"),
        P(),
        P("dp", "tensor"),
        P("tensor", None),
        P(("rep", "dp"), None, None),
        P("tensor", "dp"),
        P(),
        P("dp", "tensor"),
        P("rep"),
        P(("rep", "dp")),
        P("rep"),
    )
    return jax.shard_map(
        per_device,
        mesh=mesh,
        in_specs=placed,
        out_specs=(P(("rep", "dp"), "tensor"), P(("rep", "dp"))),
        check_vma=False,
    )
```

```python
import functools

import jax
import jax.numpy as jnp
from jax import lax
from jax.experimental import pallas as pl
from jax.experimental.pallas import tpu as pltpu
from jax.sharding import PartitionSpec as P

HEAD = 128
QH_DEV = 2
GROUP = 16
SIDE = 2


EPS = 1e-05
VMEM_LIMIT = 48 * 1024 * 1024


def product(left, right):
    return jnp.dot(left, right, preferred_element_type=jnp.float32)


def swap_dp(value):
    return lax.ppermute(value, "dp", [(0, 1), (1, 0)])


def swap_side(value):
    count = lax.axis_size("tensor")
    return lax.ppermute(value, "tensor", [(i, i ^ 1) for i in range(count)])


def ring_step(value):
    count = lax.axis_size("tensor")
    return lax.ppermute(value, "tensor", [(i, (i + SIDE) % count) for i in range(count)])


def doubling(value, combine):
    count = lax.axis_size("tensor")
    step = 1
    while step < count:
        other = lax.ppermute(value, "tensor", [(i, i ^ step) for i in range(count)])
        value = combine(value, other, step)
        step *= 2
    return value


def sum_tensor(value):
    return doubling(value, lambda a, b, step: a + b)


def gather_blocks(block):
    blocks = []
    for k in range(lax.axis_size("tensor") // SIDE):
        if k > 0:
            block = ring_step(block)
        blocks.append(block)
        blocks.append(swap_side(block))
    return blocks


def gathered_ids():
    count = lax.axis_size("tensor")
    pos = lax.axis_index("tensor")
    ids = []
    for k in range(count // SIDE):
        held = (pos - SIDE * k + count) % count
        ids += [held, held ^ 1]
    return ids


def scattered_ids():
    count = lax.axis_size("tensor")
    pos = lax.axis_index("tensor")
    ids = []
    for k in range(count // SIDE):
        held = (pos - SIDE * (k + 1) + count) % count
        ids += [held, held ^ 1]
    return ids


def row_plan(lens_ref, seqs_count, half):
    group = lax.axis_index("dp")
    own = [lens_ref[group * seqs_count + i] for i in range(seqs_count)]
    other = [lens_ref[(1 - group) * seqs_count + i] for i in range(seqs_count)]
    busy = sum(own) > half
    light_total = jnp.where(busy, sum(other), sum(own))
    own_ends, busy_ends = [], []
    long_seq, long_start = jnp.int32(0), jnp.int32(0)
    own_end, busy_end = jnp.int32(0), jnp.int32(0)
    for i in range(seqs_count):
        length = jnp.where(busy, own[i], other[i])
        long_seq = jnp.where(length == half, i, long_seq)
        long_start = jnp.where(length == half, busy_end, long_start)
        own_end, busy_end = own_end + own[i], busy_end + length
        own_ends.append(own_end)
        busy_ends.append(busy_end)
    return busy, light_total, long_seq, long_start, own_ends, busy_ends


def rest_rows(slot, light_total, long_start, half):
    rest = slot - light_total
    return rest, rest + jnp.where(rest >= long_start, half, 0)


def pack_kernel(seqs_count, lens_ref, hidden_ref, keep_ref, send_ref, pick_ref):
    rows_count = hidden_ref.shape[0]
    half = rows_count // 2
    busy, light_total, _, long_start, _, _ = row_plan(lens_ref, seqs_count, half)
    slot = lax.broadcasted_iota(jnp.int32, (half, rows_count), 0)
    row = lax.broadcasted_iota(jnp.int32, (half, rows_count), 1)
    rest, rest_row = rest_rows(slot, light_total, long_start, half)
    keep_src = jnp.where(busy, long_start + slot, jnp.where(rest < 0, slot, -1))
    send_src = jnp.where(busy & (rest >= 0), rest_row, -1)
    keep_pick = jnp.where(keep_src == row, 1.0, 0.0).astype(jnp.bfloat16)
    send_pick = jnp.where(send_src == row, 1.0, 0.0).astype(jnp.bfloat16)
    pick_ref[:half] = keep_pick
    pick_ref[half:] = send_pick
    hidden = hidden_ref[...]
    send_ref[...] = product(send_pick, hidden).astype(jnp.bfloat16)
    keep_ref[...] = product(keep_pick, hidden).astype(jnp.bfloat16)


def pack(resp_len, hidden, seqs_count):
    rows_count, shard = hidden.shape
    half = rows_count // 2
    vmem = pl.BlockSpec(memory_space=pltpu.VMEM)
    return pl.pallas_call(
        functools.partial(pack_kernel, seqs_count),
        out_shape=[
            jax.ShapeDtypeStruct((half, shard), jnp.bfloat16),
            jax.ShapeDtypeStruct((half, shard), jnp.bfloat16),
            jax.ShapeDtypeStruct((rows_count, rows_count), jnp.bfloat16),
        ],
        in_specs=[pl.BlockSpec(memory_space=pltpu.SMEM), vmem],
        out_specs=[vmem] * 3,
        compiler_params=pltpu.CompilerParams(vmem_limit_bytes=VMEM_LIMIT),
        name="pack_rows",
    )(resp_len, hidden)


def block_copies(ids, axis, own_ref, other_ref, held, sems):
    count = lax.axis_size("tensor")
    group = lax.axis_index("dp")
    size = own_ref.shape[axis] * 2 // count
    copies = []
    for j, block in enumerate(ids):
        place = pl.ds(pl.multiple_of((block % (count // 2)) * size, size), size)
        at = (place, slice(None)) if axis == 0 else (slice(None), place)
        here = pltpu.make_async_copy(own_ref.at[at], held.at[j], sems.at[j])
        there = pltpu.make_async_copy(other_ref.at[at], held.at[j], sems.at[j])
        copies.append((block // (count // 2) == group, here, there))
    return copies


def start_copies(copies):
    for is_here, here, there in copies:
        pl.when(is_here)(here.start)
        pl.when(jnp.logical_not(is_here))(there.start)


def attention_kernel(
    seqs_count,
    count,
    lens_ref,
    ctx_ref,
    gain_ref,
    kv_ref,
    q_own,
    q_other,
    cache_own,
    cache_other,
    out_own,
    out_other,
    *refs,
):
    blocks, outs = refs[:count], refs[count : 2 * count]
    q_held, cache_held, out_held, q_sems, cache_sems, out_sems = refs[2 * count :]
    half, shard = blocks[0].shape
    ctx_slots = cache_own.shape[1]
    ids = gathered_ids()
    q_copies = block_copies(ids, 0, q_own, q_other, q_held, q_sems)
    out_copies = block_copies(scattered_ids(), 1, out_own, out_other, out_held, out_sems)
    cache_copies = [
        pltpu.make_async_copy(cache_own, cache_held.at[0], cache_sems.at[0]),
        pltpu.make_async_copy(cache_other, cache_held.at[1], cache_sems.at[1]),
    ]
    start_copies(q_copies)
    for copy in cache_copies:
        copy.start()
    start_copies(out_copies)

    squares = jnp.zeros((half, 1), jnp.float32)
    for block in blocks:
        values = block[...].astype(jnp.float32)
        squares += jnp.sum(values * values, axis=1, keepdims=True)
    scale = lax.rsqrt(squares / (shard * count) + EPS)
    query = jnp.zeros((half, q_own.shape[1]), jnp.float32)
    for j, block in enumerate(blocks):
        gain = gain_ref[pl.ds(ids[j], 1), :]
        normed = (block[...].astype(jnp.float32) * scale * gain).astype(jnp.bfloat16)
        q_copies[j][1].wait()
        query += product(normed, q_held[j])
    query = query.astype(jnp.bfloat16)
    new_kv = (kv_ref[...] * scale).astype(jnp.bfloat16)

    busy, light_total, long_seq, long_start, own_ends, busy_ends = row_plan(
        lens_ref, seqs_count, half
    )
    slot = lax.broadcasted_iota(jnp.int32, (half, 1), 0)
    rest, rest_row = rest_rows(slot, light_total, long_start, half)
    own_seg, rest_seg = jnp.zeros_like(slot), jnp.full_like(slot, seqs_count)
    for i in range(seqs_count):
        own_seg += jnp.where(slot >= own_ends[i], 1, 0)
        rest_seg += jnp.where(rest_row >= busy_ends[i], 1, 0)
    seg = jnp.where(busy, long_seq, jnp.where(rest < 0, own_seg, rest_seg))
    position = lax.broadcasted_iota(jnp.int32, (half, ctx_slots), 1)
    ctx_ok = jnp.concatenate(
        [(seg == i) & (position < ctx_ref[i]) for i in range(2 * seqs_count)], axis=1
    )
    slot_b = lax.broadcasted_iota(jnp.int32, (half, half), 1)
    rest_b, rest_row_b = rest_rows(slot_b, light_total, long_start, half)
    own_seg_b, rest_seg_b = jnp.zeros_like(slot_b), jnp.full_like(slot_b, seqs_count)
    for i in range(seqs_count):
        own_seg_b += jnp.where(slot_b >= own_ends[i], 1, 0)
        rest_seg_b += jnp.where(rest_row_b >= busy_ends[i], 1, 0)
    seg_b = jnp.where(busy, long_seq, jnp.where(rest_b < 0, own_seg_b, rest_seg_b))
    own_ok = (seg_b == seg) & (slot_b <= slot)

    for copy in cache_copies:
        copy.wait()
    keys = cache_held[:, :, :, :HEAD].reshape(-1, HEAD)
    vals = cache_held[:, :, :, HEAD:].reshape(-1, HEAD)
    heads = []
    for h in range(QH_DEV):
        own_query = query[:, h * HEAD : (h + 1) * HEAD]
        contract = (((1,), (1,)), ((), ()))
        ctx_scores = lax.dot_general(own_query, keys, contract, preferred_element_type=jnp.float32)
        own_scores = lax.dot_general(
            own_query, new_kv[:, :HEAD], contract, preferred_element_type=jnp.float32
        )
        ctx_scores = jnp.where(ctx_ok, ctx_scores * HEAD ** (-0.5), -jnp.inf)
        own_scores = jnp.where(own_ok, own_scores * HEAD ** (-0.5), -jnp.inf)
        top = jnp.maximum(
            jnp.max(ctx_scores, axis=1, keepdims=True), jnp.max(own_scores, axis=1, keepdims=True)
        )
        ctx_weights, own_weights = jnp.exp(ctx_scores - top), jnp.exp(own_scores - top)
        total = jnp.sum(ctx_weights, axis=1, keepdims=True) + jnp.sum(
            own_weights, axis=1, keepdims=True
        )
        heads.append(
            product((ctx_weights / total).astype(jnp.bfloat16), vals)
            + product((own_weights / total).astype(jnp.bfloat16), new_kv[:, HEAD:])
        )
    attn = jnp.concatenate(heads, axis=1).astype(jnp.bfloat16)
    for j, out in enumerate(outs):
        out_copies[j][1].wait()
        out[...] = product(attn, out_held[j]).astype(jnp.bfloat16)


def attend(resp_len, both_ctx, attn_gain, kv_sum, q_pair, cache_pair, out_pair, blocks):
    count = len(blocks)
    half, shard = blocks[0].shape
    seqs_count, ctx_slots, width = cache_pair[0].shape
    q_width, attn_width = q_pair[0].shape[1], out_pair[0].shape[0]
    vmem = pl.BlockSpec(memory_space=pltpu.VMEM)
    smem = pl.BlockSpec(memory_space=pltpu.SMEM)
    anywhere = pl.BlockSpec(memory_space=pl.ANY)
    return pl.pallas_call(
        functools.partial(attention_kernel, seqs_count, count),
        out_shape=[jax.ShapeDtypeStruct((half, shard), jnp.bfloat16)] * count,
        in_specs=[smem] * 2 + [vmem] * 2 + [anywhere] * 6 + [vmem] * count,
        out_specs=[vmem] * count,
        scratch_shapes=[
            pltpu.VMEM((count, shard, q_width), jnp.bfloat16),
            pltpu.VMEM((2, seqs_count, ctx_slots, width), jnp.bfloat16),
            pltpu.VMEM((count, attn_width, shard), jnp.bfloat16),
            pltpu.SemaphoreType.DMA((count,)),
            pltpu.SemaphoreType.DMA((2,)),
            pltpu.SemaphoreType.DMA((count,)),
        ],
        compiler_params=pltpu.CompilerParams(vmem_limit_bytes=VMEM_LIMIT),
        name="attend",
    )(resp_len, both_ctx, attn_gain.reshape(count, shard), kv_sum, *q_pair, *cache_pair, *out_pair, *blocks)


def vocab_kernel(count, targets_ref, squares_ref, own_ref, other_ref, *refs):
    blocks, (stats_ref, held, sems) = refs[:count], refs[count:]
    half, shard = blocks[0].shape
    copies = block_copies(gathered_ids(), 0, own_ref, other_ref, held, sems)
    start_copies(copies)
    scale = lax.rsqrt(squares_ref[...] / (shard * count) + EPS)
    vocab_count = own_ref.shape[1]
    logits = jnp.zeros((half, vocab_count), jnp.float32)
    for j, block in enumerate(blocks):
        copies[j][1].wait()
        logits += product(block[...], held[j])
    logits = logits * scale
    column_ids = lax.axis_index("tensor") * vocab_count + lax.broadcasted_iota(
        jnp.int32, (half, vocab_count), 1
    )
    picked = jnp.sum(
        jnp.where(column_ids == targets_ref[...], logits, 0.0), axis=1, keepdims=True
    )
    top = jnp.max(logits, axis=1, keepdims=True)
    total = jnp.sum(jnp.exp(logits - top), axis=1, keepdims=True)
    lane = lax.broadcasted_iota(jnp.int32, (half, half), 1)
    stats = jnp.where(lane == 0, top, jnp.where(lane == 1, total, picked))
    stats_ref[...] = jnp.transpose(stats)[:8]


def vocab_stats(targets, square_sum, vocab_pair, blocks):
    count = len(blocks)
    half, shard = blocks[0].shape
    vocab_count = vocab_pair[0].shape[1]
    vmem = pl.BlockSpec(memory_space=pltpu.VMEM)
    anywhere = pl.BlockSpec(memory_space=pl.ANY)
    return pl.pallas_call(
        functools.partial(vocab_kernel, count),
        out_shape=jax.ShapeDtypeStruct((8, half), jnp.float32),
        in_specs=[vmem] * 2 + [anywhere] * 2 + [vmem] * count,
        out_specs=vmem,
        scratch_shapes=[
            pltpu.VMEM((count, shard, vocab_count), jnp.bfloat16),
            pltpu.SemaphoreType.DMA((count,)),
        ],
        compiler_params=pltpu.CompilerParams(vmem_limit_bytes=VMEM_LIMIT),
        name="vocab_stats",
    )(targets.reshape(half, 1), square_sum.reshape(half, 1), *vocab_pair, *blocks)


def per_device(
    hidden,
    attn_gain,
    q_weight,
    kv_weight,
    kv_cache,
    out_weight,
    final_gain,
    vocab_weight,
    resp_len,
    ctx_len,
    target_ids,
):
    rows_count, shard = hidden.shape
    half = rows_count // 2
    tensor_count = lax.axis_size("tensor")
    tensor_pos = lax.axis_index("tensor")
    group = lax.axis_index("dp")
    seqs_count = kv_cache.shape[0]

    keep, send, pick = pack(resp_len, hidden, seqs_count)
    rows = keep + swap_dp(send)
    rows_f = rows.astype(jnp.float32)
    blocks = gather_blocks(rows)

    gain = lax.dynamic_slice_in_dim(attn_gain, tensor_pos * shard, shard, 0)
    kv_head = tensor_pos * QH_DEV // GROUP
    kv_partial = product((rows_f * gain).astype(jnp.bfloat16), kv_weight)
    kv_sum = lax.dynamic_slice_in_dim(sum_tensor(kv_partial), kv_head * 2 * HEAD, 2 * HEAD, 1)
    cache = lax.dynamic_slice_in_dim(kv_cache, kv_head * 2 * HEAD, 2 * HEAD, 2)
    both_ctx = jnp.concatenate([ctx_len, swap_dp(ctx_len)], axis=0)
    products = attend(
        resp_len,
        both_ctx,
        attn_gain,
        kv_sum,
        (q_weight, swap_dp(q_weight)),
        (cache, swap_dp(cache)),
        (out_weight, swap_dp(out_weight)),
        blocks,
    )

    partial = None
    for k in range(tensor_count // SIDE):
        total = products[2 * k].astype(jnp.float32) + swap_side(products[2 * k + 1]).astype(jnp.float32)
        if partial is not None:
            total = total + ring_step(partial).astype(jnp.float32)
        partial = total.astype(jnp.bfloat16)
    mixed = rows_f + total

    gain = lax.dynamic_slice_in_dim(final_gain, tensor_pos * shard, shard, 0)
    blocks = gather_blocks((mixed * gain).astype(jnp.bfloat16))
    square_sum = sum_tensor(jnp.sum(mixed * mixed, axis=1)[None, :])[0]
    layer_rows = mixed.astype(jnp.bfloat16)
    layer_rows = jnp.concatenate([layer_rows, swap_dp(layer_rows)], axis=0)
    layer_out = lax.dot_general(
        pick, layer_rows, (((0,), (0,)), ((), ())), preferred_element_type=jnp.float32
    ).astype(jnp.bfloat16)

    own_targets = lax.dynamic_slice_in_dim(target_ids, group * rows_count, rows_count, 0)
    sent_targets = jnp.sum(jnp.where(pick > 0, own_targets[None, :], 0), axis=1)
    targets = sent_targets[:half] + swap_dp(sent_targets[None, half:])[0]
    stats = vocab_stats(targets, square_sum, (vocab_weight, swap_dp(vocab_weight)), blocks)

    def join(a, b, step):
        first = (tensor_pos // step) % 2 == 0
        a, b = jnp.where(first, a, b), jnp.where(first, b, a)
        top = jnp.maximum(a[0], b[0])
        total = a[1] * jnp.exp(a[0] - top) + b[1] * jnp.exp(b[0] - top)
        return jnp.stack([top, total, a[2] + b[2]])

    top, total, picked = doubling(stats[:3], join)
    logprob = (picked - top - jnp.log(total))[None, :]
    both_logprob = jnp.concatenate([logprob, swap_dp(logprob)], axis=1)
    token_logprob = jnp.sum(jnp.where(pick > 0, both_logprob.reshape(-1, 1), 0.0), axis=0)
    return (layer_out, token_logprob)


def solution(mesh):
    placed = (
        P(("rep", "dp"), "tensor"),
        P(),
        P("dp", "tensor"),
        P("tensor", None),
        P(("rep", "dp"), None, None),
        P("tensor", "dp"),
        P(),
        P("dp", "tensor"),
        P("rep"),
        P(("rep", "dp")),
        P("rep"),
    )
    return jax.shard_map(
        per_device,
        mesh=mesh,
        in_specs=placed,
        out_specs=(P(("rep", "dp"), "tensor"), P(("rep", "dp"))),
        check_vma=False,
    )
```

```python
import functools

import jax
import jax.numpy as jnp
from jax import lax
from jax.experimental import pallas as pl
from jax.experimental.pallas import tpu as pltpu
from jax.sharding import PartitionSpec as P

HEAD = 128
QH_DEV = 2
GROUP = 16
SIDE = 2


EPS = 1e-05
VMEM_LIMIT = 48 * 1024 * 1024


def product(left, right):
    return jnp.dot(left, right, preferred_element_type=jnp.float32)


def swap_dp(value):
    return lax.ppermute(value, "dp", [(0, 1), (1, 0)])


def swap_side(value):
    count = lax.axis_size("tensor")
    return lax.ppermute(value, "tensor", [(i, i ^ 1) for i in range(count)])


def ring_step(value):
    count = lax.axis_size("tensor")
    return lax.ppermute(value, "tensor", [(i, (i + SIDE) % count) for i in range(count)])


def doubling(value, combine):
    count = lax.axis_size("tensor")
    step = 1
    while step < count:
        other = lax.ppermute(value, "tensor", [(i, i ^ step) for i in range(count)])
        value = combine(value, other, step)
        step *= 2
    return value


def sum_tensor(value):
    return doubling(value, lambda a, b, step: a + b)


def after(value, *others):
    return lax.optimization_barrier((value, *others))[0]


def gather_blocks(block, beside=()):
    count = lax.axis_size("tensor") // SIDE
    blocks, values = [], []
    for k in range(count):
        crossed = swap_side(block)
        blocks += [block, crossed]
        ready = beside[k](block) if k < len(beside) else []
        values += ready
        if k + 1 < count:
            block = after(ring_step(block), crossed, *ready)
    return blocks, values


def gathered_ids():
    count = lax.axis_size("tensor")
    pos = lax.axis_index("tensor")
    ids = []
    for k in range(count // SIDE):
        held = (pos - SIDE * k + count) % count
        ids += [held, held ^ 1]
    return ids


def scattered_ids():
    count = lax.axis_size("tensor")
    pos = lax.axis_index("tensor")
    ids = []
    for k in range(count // SIDE):
        held = (pos - SIDE * (k + 1) + count) % count
        ids += [held, held ^ 1]
    return ids


def row_plan(lens_ref, seqs_count, half):
    group = lax.axis_index("dp")
    own = [lens_ref[group * seqs_count + i] for i in range(seqs_count)]
    other = [lens_ref[(1 - group) * seqs_count + i] for i in range(seqs_count)]
    busy = sum(own) > half
    light_total = jnp.where(busy, sum(other), sum(own))
    own_ends, busy_ends = [], []
    long_seq, long_start = jnp.int32(0), jnp.int32(0)
    own_end, busy_end = jnp.int32(0), jnp.int32(0)
    for i in range(seqs_count):
        length = jnp.where(busy, own[i], other[i])
        long_seq = jnp.where(length == half, i, long_seq)
        long_start = jnp.where(length == half, busy_end, long_start)
        own_end, busy_end = own_end + own[i], busy_end + length
        own_ends.append(own_end)
        busy_ends.append(busy_end)
    return busy, light_total, long_seq, long_start, own_ends, busy_ends


def rest_rows(slot, light_total, long_start, half):
    rest = slot - light_total
    return rest, rest + jnp.where(rest >= long_start, half, 0)


def pack_kernel(seqs_count, lens_ref, hidden_ref, keep_ref, send_ref, pick_ref):
    rows_count = hidden_ref.shape[0]
    half = rows_count // 2
    busy, light_total, _, long_start, _, _ = row_plan(lens_ref, seqs_count, half)
    slot = lax.broadcasted_iota(jnp.int32, (half, rows_count), 0)
    row = lax.broadcasted_iota(jnp.int32, (half, rows_count), 1)
    rest, rest_row = rest_rows(slot, light_total, long_start, half)
    keep_src = jnp.where(busy, long_start + slot, jnp.where(rest < 0, slot, -1))
    send_src = jnp.where(busy & (rest >= 0), rest_row, -1)
    keep_pick = jnp.where(keep_src == row, 1.0, 0.0).astype(jnp.bfloat16)
    send_pick = jnp.where(send_src == row, 1.0, 0.0).astype(jnp.bfloat16)
    pick_ref[:half] = keep_pick
    pick_ref[half:] = send_pick
    hidden = hidden_ref[...]
    send_ref[...] = product(send_pick, hidden).astype(jnp.bfloat16)
    keep_ref[...] = product(keep_pick, hidden).astype(jnp.bfloat16)


def pack(resp_len, hidden, seqs_count):
    rows_count, shard = hidden.shape
    half = rows_count // 2
    vmem = pl.BlockSpec(memory_space=pltpu.VMEM)
    return pl.pallas_call(
        functools.partial(pack_kernel, seqs_count),
        out_shape=[
            jax.ShapeDtypeStruct((half, shard), jnp.bfloat16),
            jax.ShapeDtypeStruct((half, shard), jnp.bfloat16),
            jax.ShapeDtypeStruct((rows_count, rows_count), jnp.bfloat16),
        ],
        in_specs=[pl.BlockSpec(memory_space=pltpu.SMEM), vmem],
        out_specs=[vmem] * 3,
        compiler_params=pltpu.CompilerParams(vmem_limit_bytes=VMEM_LIMIT),
        name="pack_rows",
    )(resp_len, hidden)


def block_copies(ids, axis, own_ref, other_ref, held, sems):
    count = lax.axis_size("tensor")
    group = lax.axis_index("dp")
    size = own_ref.shape[axis] * 2 // count
    copies = []
    for j, block in enumerate(ids):
        place = pl.ds(pl.multiple_of((block % (count // 2)) * size, size), size)
        at = (place, slice(None)) if axis == 0 else (slice(None), place)
        here = pltpu.make_async_copy(own_ref.at[at], held.at[j], sems.at[j])
        there = pltpu.make_async_copy(other_ref.at[at], held.at[j], sems.at[j])
        copies.append((block // (count // 2) == group, here, there))
    return copies


def start_copies(copies):
    for is_here, here, there in copies:
        pl.when(is_here)(here.start)
        pl.when(jnp.logical_not(is_here))(there.start)


def attention_kernel(
    seqs_count,
    count,
    lens_ref,
    ctx_ref,
    gain_ref,
    q_own,
    q_other,
    cache_own,
    cache_other,
    out_own,
    out_other,
    *refs,
):
    blocks, outs = refs[:count], refs[count : 2 * count]
    q_held, cache_held, out_held, q_sems, cache_sems, out_sems = refs[2 * count :]
    half, shard = outs[0].shape
    ctx_slots = cache_own.shape[1]
    ids = gathered_ids()
    q_copies = block_copies(ids, 0, q_own, q_other, q_held, q_sems)
    out_copies = block_copies(scattered_ids(), 1, out_own, out_other, out_held, out_sems)
    cache_copies = [
        pltpu.make_async_copy(cache_own, cache_held.at[0], cache_sems.at[0]),
        pltpu.make_async_copy(cache_other, cache_held.at[1], cache_sems.at[1]),
    ]
    start_copies(q_copies)
    for copy in cache_copies:
        copy.start()
    start_copies(out_copies)

    squares = jnp.zeros((half, 1), jnp.float32)
    for block in blocks:
        values = block[:, :shard].astype(jnp.float32)
        squares += jnp.sum(values * values, axis=1, keepdims=True)
    scale = lax.rsqrt(squares / (shard * count) + EPS)
    query = jnp.zeros((half, q_own.shape[1]), jnp.float32)
    for j, block in enumerate(blocks):
        gain = gain_ref[pl.ds(ids[j], 1), :]
        normed = (block[:, :shard].astype(jnp.float32) * scale * gain).astype(jnp.bfloat16)
        q_copies[j][1].wait()
        query += product(normed, q_held[j])
    query = query.astype(jnp.bfloat16)
    kv_head = lax.axis_index("tensor") * QH_DEV // GROUP
    kv_place = pl.ds(pl.multiple_of(shard + kv_head * 2 * HEAD, 2 * HEAD), 2 * HEAD)
    kv_sum = jnp.zeros((half, 2 * HEAD), jnp.float32)
    for block in blocks:
        kv_sum += block[:, kv_place].astype(jnp.float32)
    new_kv = (kv_sum * scale).astype(jnp.bfloat16)

    busy, light_total, long_seq, long_start, own_ends, busy_ends = row_plan(
        lens_ref, seqs_count, half
    )
    slot = lax.broadcasted_iota(jnp.int32, (half, 1), 0)
    rest, rest_row = rest_rows(slot, light_total, long_start, half)
    own_seg, rest_seg = jnp.zeros_like(slot), jnp.full_like(slot, seqs_count)
    for i in range(seqs_count):
        own_seg += jnp.where(slot >= own_ends[i], 1, 0)
        rest_seg += jnp.where(rest_row >= busy_ends[i], 1, 0)
    seg = jnp.where(busy, long_seq, jnp.where(rest < 0, own_seg, rest_seg))
    position = lax.broadcasted_iota(jnp.int32, (half, ctx_slots), 1)
    ctx_ok = jnp.concatenate(
        [(seg == i) & (position < ctx_ref[i]) for i in range(2 * seqs_count)], axis=1
    )
    slot_b = lax.broadcasted_iota(jnp.int32, (half, half), 1)
    rest_b, rest_row_b = rest_rows(slot_b, light_total, long_start, half)
    own_seg_b, rest_seg_b = jnp.zeros_like(slot_b), jnp.full_like(slot_b, seqs_count)
    for i in range(seqs_count):
        own_seg_b += jnp.where(slot_b >= own_ends[i], 1, 0)
        rest_seg_b += jnp.where(rest_row_b >= busy_ends[i], 1, 0)
    seg_b = jnp.where(busy, long_seq, jnp.where(rest_b < 0, own_seg_b, rest_seg_b))
    own_ok = (seg_b == seg) & (slot_b <= slot)

    for copy in cache_copies:
        copy.wait()
    keys = cache_held[:, :, :, :HEAD].reshape(-1, HEAD)
    vals = cache_held[:, :, :, HEAD:].reshape(-1, HEAD)
    heads = []
    for h in range(QH_DEV):
        own_query = query[:, h * HEAD : (h + 1) * HEAD]
        contract = (((1,), (1,)), ((), ()))
        ctx_scores = lax.dot_general(own_query, keys, contract, preferred_element_type=jnp.float32)
        own_scores = lax.dot_general(
            own_query, new_kv[:, :HEAD], contract, preferred_element_type=jnp.float32
        )
        ctx_scores = jnp.where(ctx_ok, ctx_scores * HEAD ** (-0.5), -jnp.inf)
        own_scores = jnp.where(own_ok, own_scores * HEAD ** (-0.5), -jnp.inf)
        top = jnp.maximum(
            jnp.max(ctx_scores, axis=1, keepdims=True), jnp.max(own_scores, axis=1, keepdims=True)
        )
        ctx_weights, own_weights = jnp.exp(ctx_scores - top), jnp.exp(own_scores - top)
        total = jnp.sum(ctx_weights, axis=1, keepdims=True) + jnp.sum(
            own_weights, axis=1, keepdims=True
        )
        heads.append(
            product((ctx_weights / total).astype(jnp.bfloat16), vals)
            + product((own_weights / total).astype(jnp.bfloat16), new_kv[:, HEAD:])
        )
    attn = jnp.concatenate(heads, axis=1).astype(jnp.bfloat16)
    for j, out in enumerate(outs):
        out_copies[j][1].wait()
        out[...] = product(attn, out_held[j]).astype(jnp.bfloat16)


def attend(resp_len, both_ctx, attn_gain, q_pair, cache_pair, out_pair, blocks):
    count = len(blocks)
    half, shard = blocks[0].shape[0], attn_gain.shape[0] // count
    seqs_count, ctx_slots, width = cache_pair[0].shape
    q_width, attn_width = q_pair[0].shape[1], out_pair[0].shape[0]
    vmem = pl.BlockSpec(memory_space=pltpu.VMEM)
    smem = pl.BlockSpec(memory_space=pltpu.SMEM)
    anywhere = pl.BlockSpec(memory_space=pl.ANY)
    return pl.pallas_call(
        functools.partial(attention_kernel, seqs_count, count),
        out_shape=[jax.ShapeDtypeStruct((half, shard), jnp.bfloat16)] * count,
        in_specs=[smem] * 2 + [vmem] + [anywhere] * 6 + [vmem] * count,
        out_specs=[vmem] * count,
        scratch_shapes=[
            pltpu.VMEM((count, shard, q_width), jnp.bfloat16),
            pltpu.VMEM((2, seqs_count, ctx_slots, width), jnp.bfloat16),
            pltpu.VMEM((count, attn_width, shard), jnp.bfloat16),
            pltpu.SemaphoreType.DMA((count,)),
            pltpu.SemaphoreType.DMA((2,)),
            pltpu.SemaphoreType.DMA((count,)),
        ],
        compiler_params=pltpu.CompilerParams(vmem_limit_bytes=VMEM_LIMIT),
        name="attend",
    )(resp_len, both_ctx, attn_gain.reshape(count, shard), *q_pair, *cache_pair, *out_pair, *blocks)


def vocab_kernel(count, targets_ref, gain_ref, own_ref, other_ref, *refs):
    blocks, (stats_ref, held, sems) = refs[:count], refs[count:]
    half, shard = blocks[0].shape
    ids = gathered_ids()
    copies = block_copies(ids, 0, own_ref, other_ref, held, sems)
    start_copies(copies)
    vocab_count = own_ref.shape[1]
    logits = jnp.zeros((half, vocab_count), jnp.float32)
    squares = jnp.zeros((half, 1), jnp.float32)
    for j, block in enumerate(blocks):
        copies[j][1].wait()
        values = block[...]
        logits += product(values, held[j])
        mixed = values.astype(jnp.float32) / gain_ref[pl.ds(ids[j], 1), :]
        squares += jnp.sum(mixed * mixed, axis=1, keepdims=True)
    scale = lax.rsqrt(squares / (shard * count) + EPS)
    logits = logits * scale
    column_ids = lax.axis_index("tensor") * vocab_count + lax.broadcasted_iota(
        jnp.int32, (half, vocab_count), 1
    )
    picked = jnp.sum(
        jnp.where(column_ids == targets_ref[...], logits, 0.0), axis=1, keepdims=True
    )
    top = jnp.max(logits, axis=1, keepdims=True)
    total = jnp.sum(jnp.exp(logits - top), axis=1, keepdims=True)
    lane = lax.broadcasted_iota(jnp.int32, (half, half), 1)
    stats = jnp.where(lane == 0, top, jnp.where(lane == 1, total, picked))
    stats_ref[...] = jnp.transpose(stats)[:8]


def vocab_stats(targets, final_gain, vocab_pair, blocks):
    count = len(blocks)
    half, shard = blocks[0].shape
    vocab_count = vocab_pair[0].shape[1]
    vmem = pl.BlockSpec(memory_space=pltpu.VMEM)
    anywhere = pl.BlockSpec(memory_space=pl.ANY)
    return pl.pallas_call(
        functools.partial(vocab_kernel, count),
        out_shape=jax.ShapeDtypeStruct((8, half), jnp.float32),
        in_specs=[vmem] * 2 + [anywhere] * 2 + [vmem] * count,
        out_specs=vmem,
        scratch_shapes=[
            pltpu.VMEM((count, shard, vocab_count), jnp.bfloat16),
            pltpu.SemaphoreType.DMA((count,)),
        ],
        compiler_params=pltpu.CompilerParams(vmem_limit_bytes=VMEM_LIMIT),
        name="vocab_stats",
    )(targets.reshape(half, 1), final_gain.reshape(count, shard), *vocab_pair, *blocks)


def per_device(
    hidden,
    attn_gain,
    q_weight,
    kv_weight,
    kv_cache,
    out_weight,
    final_gain,
    vocab_weight,
    resp_len,
    ctx_len,
    target_ids,
):
    rows_count, shard = hidden.shape
    half = rows_count // 2
    tensor_count = lax.axis_size("tensor")
    tensor_pos = lax.axis_index("tensor")
    group = lax.axis_index("dp")
    seqs_count = kv_cache.shape[0]

    keep, send, pick = pack(resp_len, hidden, seqs_count)
    rows = keep + swap_dp(send)
    rows_f = rows.astype(jnp.float32)

    gain = lax.dynamic_slice_in_dim(attn_gain, tensor_pos * shard, shard, 0)
    kv_partial = product((rows_f * gain).astype(jnp.bfloat16), kv_weight)
    cache = kv_cache
    if kv_cache.shape[2] != 2 * HEAD:
        kv_head = tensor_pos * QH_DEV // GROUP
        cache = lax.dynamic_slice_in_dim(kv_cache, kv_head * 2 * HEAD, 2 * HEAD, 2)
    def swap_rest(block):
        context = after(ctx_len, block)
        own_targets = lax.dynamic_slice_in_dim(
            after(target_ids, block), group * rows_count, rows_count, 0
        )
        sent_targets = jnp.sum(jnp.where(pick > 0, own_targets[None, :], 0), axis=1)
        return [
            swap_dp(after(cache, block)),
            jnp.concatenate([ctx_len, swap_dp(context)], axis=0),
            sent_targets[:half] + swap_dp(sent_targets[None, half:])[0],
        ]

    blocks, values = gather_blocks(
        jnp.concatenate([rows, kv_partial.astype(jnp.bfloat16)], axis=1),
        [
            lambda block: [swap_dp(after(q_weight, block))],
            lambda block: [swap_dp(after(out_weight, block))],
            swap_rest,
        ],
    )
    q_other, out_other, cache_other, both_ctx, targets = values
    products = attend(
        resp_len,
        both_ctx,
        attn_gain,
        (q_weight, q_other),
        (cache, cache_other),
        (out_weight, out_other),
        blocks,
    )

    partial = None
    for k in range(tensor_count // SIDE):
        total = products[2 * k].astype(jnp.float32) + swap_side(products[2 * k + 1]).astype(jnp.float32)
        if partial is not None:
            total = total + ring_step(partial).astype(jnp.float32)
        partial = total.astype(jnp.bfloat16)
    mixed = rows_f + total

    gain = lax.dynamic_slice_in_dim(final_gain, tensor_pos * shard, shard, 0)

    def place_rows(block):
        layer_rows = mixed.astype(jnp.bfloat16)
        layer_rows = jnp.concatenate([layer_rows, swap_dp(layer_rows)], axis=0)
        return [
            lax.dot_general(
                pick, layer_rows, (((0,), (0,)), ((), ())), preferred_element_type=jnp.float32
            ).astype(jnp.bfloat16)
        ]

    blocks, (layer_out, vocab_other) = gather_blocks(
        (mixed * gain).astype(jnp.bfloat16),
        [place_rows, lambda block: [swap_dp(after(vocab_weight, block))]],
    )
    stats = vocab_stats(targets, final_gain, (vocab_weight, vocab_other), blocks)

    def join(a, b, step):
        first = (tensor_pos // step) % 2 == 0
        a, b = jnp.where(first, a, b), jnp.where(first, b, a)
        top = jnp.maximum(a[0], b[0])
        total = a[1] * jnp.exp(a[0] - top) + b[1] * jnp.exp(b[0] - top)
        return jnp.stack([top, total, a[2] + b[2]])

    top, total, picked = doubling(stats[:3], join)
    logprob = (picked - top - jnp.log(total))[None, :]
    both_logprob = jnp.concatenate([logprob, swap_dp(logprob)], axis=1)
    token_logprob = jnp.sum(jnp.where(pick > 0, both_logprob.reshape(-1, 1), 0.0), axis=0)
    return (layer_out, token_logprob)


def solution(mesh):
    placed = (
        P(("rep", "dp"), "tensor"),
        P(),
        P("dp", "tensor"),
        P("tensor", None),
        P(("rep", "dp"), None, None),
        P("tensor", "dp"),
        P(),
        P("dp", "tensor"),
        P("rep"),
        P(("rep", "dp")),
        P("rep"),
    )
    return jax.shard_map(
        per_device,
        mesh=mesh,
        in_specs=placed,
        out_specs=(P(("rep", "dp"), "tensor"), P(("rep", "dp"))),
        check_vma=False,
    )
```

```python
import functools

import jax
import jax.numpy as jnp
from jax import lax
from jax.experimental import pallas as pl
from jax.experimental.pallas import tpu as pltpu
from jax.sharding import PartitionSpec as P

HEAD = 128
QH_DEV = 2
GROUP = 16
SIDE = 2


EPS = 1e-05
VMEM_LIMIT = 48 * 1024 * 1024


def product(left, right):
    return jnp.dot(left, right, preferred_element_type=jnp.float32)


def swap_dp(value):
    return lax.ppermute(value, "dp", [(0, 1), (1, 0)])


def swap_side(value):
    count = lax.axis_size("tensor")
    return lax.ppermute(value, "tensor", [(i, i ^ 1) for i in range(count)])


def ring_step(value):
    count = lax.axis_size("tensor")
    return lax.ppermute(value, "tensor", [(i, (i + SIDE) % count) for i in range(count)])


def doubling(value, combine):
    count = lax.axis_size("tensor")
    step = 1
    while step < count:
        other = lax.ppermute(value, "tensor", [(i, i ^ step) for i in range(count)])
        value = combine(value, other, step)
        step *= 2
    return value


def sum_tensor(value):
    return doubling(value, lambda a, b, step: a + b)


def after(value, *others):
    return lax.optimization_barrier((value, *others))[0]


def gather_blocks(block, beside=()):
    count = lax.axis_size("tensor") // SIDE
    blocks, values = [], []
    for k in range(count):
        crossed = swap_side(block)
        blocks += [block, crossed]
        ready = beside[k](block) if k < len(beside) else []
        values += ready
        if k + 1 < count:
            block = after(ring_step(block), crossed, *ready)
    return blocks, values


def gathered_ids():
    count = lax.axis_size("tensor")
    pos = lax.axis_index("tensor")
    ids = []
    for k in range(count // SIDE):
        held = (pos - SIDE * k + count) % count
        ids += [held, held ^ 1]
    return ids


def scattered_ids():
    count = lax.axis_size("tensor")
    pos = lax.axis_index("tensor")
    ids = []
    for k in range(count // SIDE):
        held = (pos - SIDE * (k + 1) + count) % count
        ids += [held, held ^ 1]
    return ids


def row_plan(lens_ref, seqs_count, half):
    group = lax.axis_index("dp")
    own = [lens_ref[group * seqs_count + i] for i in range(seqs_count)]
    other = [lens_ref[(1 - group) * seqs_count + i] for i in range(seqs_count)]
    busy = sum(own) > half
    light_total = jnp.where(busy, sum(other), sum(own))
    own_ends, busy_ends = [], []
    long_seq, long_start = jnp.int32(0), jnp.int32(0)
    own_end, busy_end = jnp.int32(0), jnp.int32(0)
    for i in range(seqs_count):
        length = jnp.where(busy, own[i], other[i])
        long_seq = jnp.where(length == half, i, long_seq)
        long_start = jnp.where(length == half, busy_end, long_start)
        own_end, busy_end = own_end + own[i], busy_end + length
        own_ends.append(own_end)
        busy_ends.append(busy_end)
    return busy, light_total, long_seq, long_start, own_ends, busy_ends


def rest_rows(slot, light_total, long_start, half):
    rest = slot - light_total
    return rest, rest + jnp.where(rest >= long_start, half, 0)


def pack_kernel(seqs_count, lens_ref, hidden_ref, keep_ref, send_ref, pick_ref):
    rows_count = hidden_ref.shape[0]
    half = rows_count // 2
    busy, light_total, _, long_start, _, _ = row_plan(lens_ref, seqs_count, half)
    slot = lax.broadcasted_iota(jnp.int32, (half, rows_count), 0)
    row = lax.broadcasted_iota(jnp.int32, (half, rows_count), 1)
    rest, rest_row = rest_rows(slot, light_total, long_start, half)
    keep_src = jnp.where(busy, long_start + slot, jnp.where(rest < 0, slot, -1))
    send_src = jnp.where(busy & (rest >= 0), rest_row, -1)
    keep_pick = jnp.where(keep_src == row, 1.0, 0.0).astype(jnp.bfloat16)
    send_pick = jnp.where(send_src == row, 1.0, 0.0).astype(jnp.bfloat16)
    pick_ref[:half] = keep_pick
    pick_ref[half:] = send_pick
    hidden = hidden_ref[...]
    send_ref[...] = product(send_pick, hidden).astype(jnp.bfloat16)
    keep_ref[...] = product(keep_pick, hidden).astype(jnp.bfloat16)


def pack(resp_len, hidden, seqs_count):
    rows_count, shard = hidden.shape
    half = rows_count // 2
    vmem = pl.BlockSpec(memory_space=pltpu.VMEM)
    return pl.pallas_call(
        functools.partial(pack_kernel, seqs_count),
        out_shape=[
            jax.ShapeDtypeStruct((half, shard), jnp.bfloat16),
            jax.ShapeDtypeStruct((half, shard), jnp.bfloat16),
            jax.ShapeDtypeStruct((rows_count, rows_count), jnp.bfloat16),
        ],
        in_specs=[pl.BlockSpec(memory_space=pltpu.SMEM), vmem],
        out_specs=[vmem] * 3,
        compiler_params=pltpu.CompilerParams(vmem_limit_bytes=VMEM_LIMIT),
        name="pack_rows",
    )(resp_len, hidden)


def block_copies(ids, axis, own_ref, other_ref, held, sems):
    count = lax.axis_size("tensor")
    group = lax.axis_index("dp")
    size = own_ref.shape[axis] * 2 // count
    copies = []
    for j, block in enumerate(ids):
        place = pl.ds(pl.multiple_of((block % (count // 2)) * size, size), size)
        at = (place, slice(None)) if axis == 0 else (slice(None), place)
        here = pltpu.make_async_copy(own_ref.at[at], held.at[j], sems.at[j])
        there = pltpu.make_async_copy(other_ref.at[at], held.at[j], sems.at[j])
        copies.append((block // (count // 2) == group, here, there))
    return copies


def start_copies(copies):
    for is_here, here, there in copies:
        pl.when(is_here)(here.start)
        pl.when(jnp.logical_not(is_here))(there.start)


def query_blocks(blocks, shard, ids, copies, held, gain_ref, query, new_kv, squares):
    kv_head = lax.axis_index("tensor") * QH_DEV // GROUP
    kv_place = pl.ds(pl.multiple_of(shard + kv_head * 2 * HEAD, 2 * HEAD), 2 * HEAD)
    for j, block in enumerate(blocks):
        values = block[:, :shard].astype(jnp.float32)
        squares += jnp.sum(values * values, axis=1, keepdims=True)
        gained = (values * gain_ref[pl.ds(ids[j], 1), :]).astype(jnp.bfloat16)
        new_kv += block[:, kv_place].astype(jnp.float32)
        copies[j][1].wait()
        query += product(gained, held[j])
    return query, new_kv, squares


def query_kernel(shard, gain_ref, q_own, q_other, *refs):
    blocks, (query_ref, kv_ref, squares_ref, held, sems) = refs[:-5], refs[-5:]
    ids = gathered_ids()[: len(blocks)]
    copies = block_copies(ids, 0, q_own, q_other, held, sems)
    start_copies(copies)
    query, new_kv = jnp.zeros(query_ref.shape, jnp.float32), jnp.zeros(kv_ref.shape, jnp.float32)
    squares = jnp.zeros((query.shape[0], 1), jnp.float32)
    query, new_kv, squares = query_blocks(
        blocks, shard, ids, copies, held, gain_ref, query, new_kv, squares
    )
    query_ref[...] = query
    kv_ref[...] = new_kv
    squares_ref[...] = jnp.broadcast_to(squares, squares_ref.shape)


def query_part(gains, q_pair, blocks):
    shard, used, half = gains.shape[1], len(blocks), blocks[0].shape[0]
    q_width = q_pair[0].shape[1]
    vmem = pl.BlockSpec(memory_space=pltpu.VMEM)
    anywhere = pl.BlockSpec(memory_space=pl.ANY)
    return pl.pallas_call(
        functools.partial(query_kernel, shard),
        out_shape=[
            jax.ShapeDtypeStruct((half, q_width), jnp.float32),
            jax.ShapeDtypeStruct((half, 2 * HEAD), jnp.float32),
            jax.ShapeDtypeStruct((half, 128), jnp.float32),
        ],
        in_specs=[vmem] + [anywhere] * 2 + [vmem] * used,
        out_specs=[vmem] * 3,
        scratch_shapes=[
            pltpu.VMEM((used, shard, q_width), jnp.bfloat16),
            pltpu.SemaphoreType.DMA((used,)),
        ],
        compiler_params=pltpu.CompilerParams(vmem_limit_bytes=VMEM_LIMIT),
        cost_estimate=pl.CostEstimate(
            flops=2 * half * used * shard * q_width,
            bytes_accessed=2 * used * shard * (half + q_width),
            transcendentals=0,
        ),
        name="query_part",
    )(gains, *q_pair, *blocks)


def attention_kernel(
    seqs_count,
    lens_ref,
    ctx_ref,
    gain_ref,
    query_ref,
    kv_ref,
    squares_ref,
    block_ref,
    q_own,
    q_other,
    cache_own,
    cache_other,
    out_own,
    out_other,
    attn_ref,
    first_ref,
    q_held,
    cache_held,
    out_held,
    q_sems,
    cache_sems,
    out_sems,
):
    half, shard = first_ref.shape
    count = lax.axis_size("tensor")
    ctx_slots = cache_own.shape[1]
    ids = gathered_ids()[-1:]
    q_copies = block_copies(ids, 0, q_own, q_other, q_held, q_sems)
    out_copies = block_copies(scattered_ids()[1:2], 1, out_own, out_other, out_held, out_sems)
    cache_copies = [
        pltpu.make_async_copy(cache_own, cache_held.at[0], cache_sems.at[0]),
        pltpu.make_async_copy(cache_other, cache_held.at[1], cache_sems.at[1]),
    ]
    start_copies(q_copies)
    for copy in cache_copies:
        copy.start()
    start_copies(out_copies)

    query, new_kv, squares = query_blocks(
        [block_ref],
        shard,
        ids,
        q_copies,
        q_held,
        gain_ref,
        query_ref[...],
        kv_ref[...],
        squares_ref[:, :1],
    )
    scale = lax.rsqrt(squares / (shard * count) + EPS)
    query = (query * scale).astype(jnp.bfloat16)
    new_kv = (new_kv * scale).astype(jnp.bfloat16)

    busy, light_total, long_seq, long_start, own_ends, busy_ends = row_plan(
        lens_ref, seqs_count, half
    )

    def segments(slot):
        rest, rest_row = rest_rows(slot, light_total, long_start, half)
        own_seg, rest_seg = jnp.zeros_like(slot), jnp.full_like(slot, seqs_count)
        for i in range(seqs_count):
            own_seg += jnp.where(slot >= own_ends[i], 1, 0)
            rest_seg += jnp.where(rest_row >= busy_ends[i], 1, 0)
        return jnp.where(busy, long_seq, jnp.where(rest < 0, own_seg, rest_seg))

    slot = lax.broadcasted_iota(jnp.int32, (half, 1), 0)
    key_slot = lax.broadcasted_iota(jnp.int32, (1, half), 1)
    seg = segments(slot)
    own_ok = (segments(key_slot) == seg) & (key_slot <= slot)
    position = lax.broadcasted_iota(jnp.int32, (half, ctx_slots), 1)

    for copy in cache_copies:
        copy.wait()
    keys = cache_held[:, :, :, :HEAD].reshape(-1, HEAD)
    vals = cache_held[:, :, :, HEAD:].reshape(-1, HEAD)
    stacked = jnp.concatenate(
        [query[:, h * HEAD : (h + 1) * HEAD] for h in range(QH_DEV)], axis=0
    )
    contract = (((1,), (1,)), ((), ()))
    ctx_scores = lax.dot_general(stacked, keys, contract, preferred_element_type=jnp.float32)
    own_scores = lax.dot_general(
        stacked, new_kv[:, :HEAD], contract, preferred_element_type=jnp.float32
    )
    ctx_scores = ctx_scores * HEAD ** (-0.5)
    own_scores = own_scores * HEAD ** (-0.5)
    heads_ctx, heads_own = [], []
    for h in range(QH_DEV):
        rows = slice(h * half, (h + 1) * half)
        pieces = []
        for i in range(2 * seqs_count):
            allowed = (seg == i) & (position < ctx_ref[i])
            piece = ctx_scores[rows, i * ctx_slots : (i + 1) * ctx_slots]
            pieces.append(jnp.where(allowed, piece, -jnp.inf))
        scores = jnp.concatenate(pieces, axis=1)
        own = jnp.where(own_ok, own_scores[rows], -jnp.inf)
        top = jnp.maximum(
            jnp.max(scores, axis=1, keepdims=True), jnp.max(own, axis=1, keepdims=True)
        )
        weights, own_weights = jnp.exp(scores - top), jnp.exp(own - top)
        total = jnp.sum(weights, axis=1, keepdims=True) + jnp.sum(
            own_weights, axis=1, keepdims=True
        )
        heads_ctx.append((weights / total).astype(jnp.bfloat16))
        heads_own.append((own_weights / total).astype(jnp.bfloat16))
    mixed_vals = product(jnp.concatenate(heads_ctx, axis=0), vals) + product(
        jnp.concatenate(heads_own, axis=0), new_kv[:, HEAD:]
    )
    attn = jnp.concatenate(
        [mixed_vals[h * half : (h + 1) * half] for h in range(QH_DEV)], axis=1
    ).astype(jnp.bfloat16)
    attn_ref[...] = attn
    out_copies[0][1].wait()
    first_ref[...] = product(attn, out_held[0]).astype(jnp.bfloat16)


def attend(resp_len, both_ctx, gains, parts, block, q_pair, cache_pair, out_pair):
    half, shard = block.shape[0], gains.shape[1]
    seqs_count, ctx_slots, width = cache_pair[0].shape
    q_width, attn_width = q_pair[0].shape[1], out_pair[0].shape[0]
    vmem = pl.BlockSpec(memory_space=pltpu.VMEM)
    smem = pl.BlockSpec(memory_space=pltpu.SMEM)
    anywhere = pl.BlockSpec(memory_space=pl.ANY)
    return pl.pallas_call(
        functools.partial(attention_kernel, seqs_count),
        out_shape=[
            jax.ShapeDtypeStruct((half, attn_width), jnp.bfloat16),
            jax.ShapeDtypeStruct((half, shard), jnp.bfloat16),
        ],
        in_specs=[smem] * 2 + [vmem] * 5 + [anywhere] * 6,
        out_specs=[vmem] * 2,
        scratch_shapes=[
            pltpu.VMEM((1, shard, q_width), jnp.bfloat16),
            pltpu.VMEM((2, seqs_count, ctx_slots, width), jnp.bfloat16),
            pltpu.VMEM((1, attn_width, shard), jnp.bfloat16),
            pltpu.SemaphoreType.DMA((1,)),
            pltpu.SemaphoreType.DMA((2,)),
            pltpu.SemaphoreType.DMA((1,)),
        ],
        compiler_params=pltpu.CompilerParams(vmem_limit_bytes=VMEM_LIMIT),
        name="attend",
    )(resp_len, both_ctx, gains, *parts, block, *q_pair, *cache_pair, *out_pair)


def out_kernel(attn_ref, out_own, out_other, *refs):
    outs, (held, sems) = refs[:-2], refs[-2:]
    ids = scattered_ids()
    copies = block_copies(ids[:1] + ids[2:], 1, out_own, out_other, held, sems)
    start_copies(copies)
    attn = attn_ref[...]
    for j, out in enumerate(outs):
        copies[j][1].wait()
        out[...] = product(attn, held[j]).astype(jnp.bfloat16)


def out_products(attn, out_pair):
    half, attn_width = attn.shape
    count = lax.axis_size("tensor")
    shard = out_pair[0].shape[1] * 2 // count
    vmem = pl.BlockSpec(memory_space=pltpu.VMEM)
    anywhere = pl.BlockSpec(memory_space=pl.ANY)
    return pl.pallas_call(
        out_kernel,
        out_shape=[jax.ShapeDtypeStruct((half, shard), jnp.bfloat16)] * (count - 1),
        in_specs=[vmem] + [anywhere] * 2,
        out_specs=[vmem] * (count - 1),
        scratch_shapes=[
            pltpu.VMEM((count - 1, attn_width, shard), jnp.bfloat16),
            pltpu.SemaphoreType.DMA((count - 1,)),
        ],
        compiler_params=pltpu.CompilerParams(vmem_limit_bytes=VMEM_LIMIT),
        cost_estimate=pl.CostEstimate(
            flops=2 * half * (count - 1) * shard * attn_width,
            bytes_accessed=2 * (count - 1) * shard * (half + attn_width),
            transcendentals=0,
        ),
        name="out_products",
    )(attn, *out_pair)


def logit_blocks(blocks, ids, copies, held, gain_ref, logits, squares):
    for j, block in enumerate(blocks):
        values = block[...]
        mixed = values.astype(jnp.float32) / gain_ref[pl.ds(ids[j], 1), :]
        squares += jnp.sum(mixed * mixed, axis=1, keepdims=True)
        copies[j][1].wait()
        logits += product(values, held[j])
    return logits, squares


def logit_kernel(gain_ref, own_ref, other_ref, *refs):
    blocks, (logits_ref, squares_ref, held, sems) = refs[:-4], refs[-4:]
    ids = gathered_ids()[: len(blocks)]
    copies = block_copies(ids, 0, own_ref, other_ref, held, sems)
    start_copies(copies)
    logits = jnp.zeros(logits_ref.shape, jnp.float32)
    squares = jnp.zeros((logits.shape[0], 1), jnp.float32)
    logits, squares = logit_blocks(blocks, ids, copies, held, gain_ref, logits, squares)
    logits_ref[...] = logits
    squares_ref[...] = jnp.broadcast_to(squares, squares_ref.shape)


def logit_part(gains, vocab_pair, blocks):
    used, (half, shard) = len(blocks), blocks[0].shape
    vocab_count = vocab_pair[0].shape[1]
    vmem = pl.BlockSpec(memory_space=pltpu.VMEM)
    anywhere = pl.BlockSpec(memory_space=pl.ANY)
    return pl.pallas_call(
        logit_kernel,
        out_shape=[
            jax.ShapeDtypeStruct((half, vocab_count), jnp.float32),
            jax.ShapeDtypeStruct((half, 128), jnp.float32),
        ],
        in_specs=[vmem] + [anywhere] * 2 + [vmem] * used,
        out_specs=[vmem] * 2,
        scratch_shapes=[
            pltpu.VMEM((used, shard, vocab_count), jnp.bfloat16),
            pltpu.SemaphoreType.DMA((used,)),
        ],
        compiler_params=pltpu.CompilerParams(vmem_limit_bytes=VMEM_LIMIT),
        cost_estimate=pl.CostEstimate(
            flops=2 * half * used * shard * vocab_count,
            bytes_accessed=2 * used * shard * (half + vocab_count),
            transcendentals=0,
        ),
        name="logit_part",
    )(gains, *vocab_pair, *blocks)


def stats_kernel(
    targets_ref, gain_ref, logits_ref, squares_ref, block_ref, own_ref, other_ref, stats_ref, held, sems
):
    half, shard = block_ref.shape
    ids = gathered_ids()[-1:]
    copies = block_copies(ids, 0, own_ref, other_ref, held, sems)
    start_copies(copies)
    logits, squares = logit_blocks(
        [block_ref], ids, copies, held, gain_ref, logits_ref[...], squares_ref[:, :1]
    )
    logits = logits * lax.rsqrt(squares / (shard * lax.axis_size("tensor")) + EPS)
    vocab_count = logits.shape[1]
    column_ids = lax.axis_index("tensor") * vocab_count + lax.broadcasted_iota(
        jnp.int32, (half, vocab_count), 1
    )
    picked = jnp.sum(
        jnp.where(column_ids == targets_ref[...], logits, 0.0), axis=1, keepdims=True
    )
    top = jnp.max(logits, axis=1, keepdims=True)
    total = jnp.sum(jnp.exp(logits - top), axis=1, keepdims=True)
    lane = lax.broadcasted_iota(jnp.int32, (half, 128), 1)
    stats = jnp.where(lane == 0, top, jnp.where(lane == 1, total, picked))
    stats_ref[...] = jnp.transpose(stats)[:8]


def vocab_stats(targets, gains, parts, block, vocab_pair):
    half, shard = block.shape
    vocab_count = vocab_pair[0].shape[1]
    vmem = pl.BlockSpec(memory_space=pltpu.VMEM)
    anywhere = pl.BlockSpec(memory_space=pl.ANY)
    return pl.pallas_call(
        stats_kernel,
        out_shape=jax.ShapeDtypeStruct((8, half), jnp.float32),
        in_specs=[vmem] * 5 + [anywhere] * 2,
        out_specs=vmem,
        scratch_shapes=[
            pltpu.VMEM((1, shard, vocab_count), jnp.bfloat16),
            pltpu.SemaphoreType.DMA((1,)),
        ],
        compiler_params=pltpu.CompilerParams(vmem_limit_bytes=VMEM_LIMIT),
        name="vocab_stats",
    )(targets.reshape(half, 1), gains, *parts, block, *vocab_pair)


def per_device(
    hidden,
    attn_gain,
    q_weight,
    kv_weight,
    kv_cache,
    out_weight,
    final_gain,
    vocab_weight,
    resp_len,
    ctx_len,
    target_ids,
):
    rows_count, shard = hidden.shape
    half = rows_count // 2
    tensor_count = lax.axis_size("tensor")
    tensor_pos = lax.axis_index("tensor")
    group = lax.axis_index("dp")
    seqs_count = kv_cache.shape[0]

    keep, send, pick = pack(resp_len, hidden, seqs_count)
    rows = keep + swap_dp(send)
    rows_f = rows.astype(jnp.float32)

    gain = lax.dynamic_slice_in_dim(attn_gain, tensor_pos * shard, shard, 0)
    kv_partial = product((rows_f * gain).astype(jnp.bfloat16), kv_weight)
    cache = kv_cache
    if kv_cache.shape[2] != 2 * HEAD:
        kv_head = tensor_pos * QH_DEV // GROUP
        cache = lax.dynamic_slice_in_dim(kv_cache, kv_head * 2 * HEAD, 2 * HEAD, 2)
    def swap_rest(block):
        context = after(ctx_len, block)
        own_targets = lax.dynamic_slice_in_dim(
            after(target_ids, block), group * rows_count, rows_count, 0
        )
        sent_targets = jnp.sum(jnp.where(pick > 0, own_targets[None, :], 0), axis=1)
        return [
            swap_dp(after(cache, block)),
            jnp.concatenate([ctx_len, swap_dp(context)], axis=0),
            sent_targets[:half] + swap_dp(sent_targets[None, half:])[0],
        ]

    blocks, values = gather_blocks(
        jnp.concatenate([rows, kv_partial.astype(jnp.bfloat16)], axis=1),
        [
            lambda block: [swap_dp(after(q_weight, block))],
            lambda block: [swap_dp(after(out_weight, block))],
            swap_rest,
        ],
    )
    q_other, out_other, cache_other, both_ctx, targets = values
    q_pair, out_pair = (q_weight, q_other), (out_weight, out_other)
    gains = attn_gain.reshape(tensor_count, shard)
    parts = query_part(gains, q_pair, blocks[:-1])
    attn, first = attend(
        resp_len, both_ctx, gains, parts, blocks[-1], q_pair, (cache, cache_other), out_pair
    )
    products = out_products(attn, out_pair)
    products = [products[0], first, *products[1:]]

    partial = None
    for k in range(tensor_count // SIDE):
        total = products[2 * k].astype(jnp.float32) + swap_side(products[2 * k + 1]).astype(jnp.float32)
        if partial is not None:
            total = total + ring_step(partial).astype(jnp.float32)
        partial = total.astype(jnp.bfloat16)
    mixed = rows_f + total

    gain = lax.dynamic_slice_in_dim(final_gain, tensor_pos * shard, shard, 0)

    def place_rows(block):
        layer_rows = mixed.astype(jnp.bfloat16)
        layer_rows = jnp.concatenate([layer_rows, swap_dp(layer_rows)], axis=0)
        return [
            lax.dot_general(
                pick, layer_rows, (((0,), (0,)), ((), ())), preferred_element_type=jnp.float32
            ).astype(jnp.bfloat16)
        ]

    blocks, (layer_out, vocab_other) = gather_blocks(
        (mixed * gain).astype(jnp.bfloat16),
        [place_rows, lambda block: [swap_dp(after(vocab_weight, block))]],
    )
    gains = final_gain.reshape(tensor_count, shard)
    vocab_pair = (vocab_weight, vocab_other)
    parts = logit_part(gains, vocab_pair, blocks[:-1])
    stats = vocab_stats(targets, gains, parts, blocks[-1], vocab_pair)[:3]

    def join(parts):
        top = functools.reduce(jnp.maximum, [part[0] for part in parts])
        total = sum(part[1] * jnp.exp(part[0] - top) for part in parts)
        return jnp.stack([top, total, sum(part[2] for part in parts)])

    def in_order(part, others, place):
        held = [part, *others]
        return [
            functools.reduce(
                lambda a, c: jnp.where(place(c) == p, held[c], a), range(1, len(held)), held[0]
            )
            for p in range(len(held))
        ]

    side = tensor_pos % SIDE
    stats = join(in_order(stats, [swap_side(stats)], lambda c: side ^ c))
    ring_count = tensor_count // SIDE
    ring_pos = tensor_pos // SIDE
    others = [
        lax.ppermute(
            stats, "tensor", [(i, (i + SIDE * c) % tensor_count) for i in range(tensor_count)]
        )
        for c in range(1, ring_count)
    ]
    stats = join(
        in_order(stats, others, lambda c: (ring_pos - c + ring_count) % ring_count)
    )
    logprob = (stats[2] - stats[0] - jnp.log(stats[1]))[None, :]
    both_logprob = jnp.concatenate([logprob, swap_dp(logprob)], axis=1)
    token_logprob = jnp.sum(jnp.where(pick > 0, both_logprob.reshape(-1, 1), 0.0), axis=0)
    return (layer_out, token_logprob)


def solution(mesh):
    placed = (
        P(("rep", "dp"), "tensor"),
        P(),
        P("dp", "tensor"),
        P("tensor", None),
        P(("rep", "dp"), None, None),
        P("tensor", "dp"),
        P(),
        P("dp", "tensor"),
        P("rep"),
        P(("rep", "dp")),
        P("rep"),
    )
    return jax.shard_map(
        per_device,
        mesh=mesh,
        in_specs=placed,
        out_specs=(P(("rep", "dp"), "tensor"), P(("rep", "dp"))),
        check_vma=False,
    )
```

```python
import functools

import jax
import jax.numpy as jnp
from jax import lax
from jax.experimental import pallas as pl
from jax.experimental.pallas import tpu as pltpu
from jax.sharding import PartitionSpec as P

HEAD = 128
QH_DEV = 2
GROUP = 16
SIDE = 2


EPS = 1e-05
VMEM_LIMIT = 52 * 1024 * 1024


def product(left, right):
    return jnp.dot(left, right, preferred_element_type=jnp.float32)


def swap_dp(value):
    return lax.ppermute(value, "dp", [(0, 1), (1, 0)])


def swap_side(value):
    count = lax.axis_size("tensor")
    return lax.ppermute(value, "tensor", [(i, i ^ 1) for i in range(count)])


def ring_seat(seat, count):
    return jnp.where(seat == 0, 0, jnp.where(seat <= count // 2, 2 * seat - 1, 2 * (count - seat)))


def seat_of(place, count):
    return jnp.where(place % 2 == 1, (place + 1) // 2, (count - place // 2) % count)


def ring_step(value):
    count = lax.axis_size("tensor")
    ring = [0, *range(1, count // SIDE, 2), *range(count // SIDE - 2, 0, -2)]
    following = dict(zip(ring, ring[1:] + ring[:1]))
    pairs = [(i, following[i // SIDE] * SIDE + i % SIDE) for i in range(count)]
    return lax.ppermute(value, "tensor", pairs)


def after(value, *others):
    return lax.optimization_barrier((value, *others))[0]


def gather_blocks(block, beside=()):
    count = lax.axis_size("tensor") // SIDE
    blocks, values = [], []
    for k in range(count):
        crossed = swap_side(block)
        blocks += [block, crossed]
        ready = beside[k](block) if k < len(beside) else []
        values += ready
        if k + 1 < count:
            block = after(ring_step(block), crossed, *ready)
    return blocks, values


def ring_ids(first):
    count = lax.axis_size("tensor")
    pos = lax.axis_index("tensor")
    ring_count = count // SIDE
    seat = seat_of(pos // SIDE, ring_count)
    ids = []
    for k in range(first, first + ring_count):
        held = ring_seat((seat - k + 2 * ring_count) % ring_count, ring_count) * SIDE + pos % SIDE
        ids += [held, held ^ 1]
    return ids


def gathered_ids():
    return ring_ids(0)


def scattered_ids():
    return ring_ids(1)


def row_plan(lens_ref, seqs_count, half):
    group = lax.axis_index("dp")
    own = [lens_ref[group * seqs_count + i] for i in range(seqs_count)]
    other = [lens_ref[(1 - group) * seqs_count + i] for i in range(seqs_count)]
    busy = sum(own) > half
    light_total = jnp.where(busy, sum(other), sum(own))
    own_ends, busy_ends = [], []
    long_seq, long_start = jnp.int32(0), jnp.int32(0)
    own_end, busy_end = jnp.int32(0), jnp.int32(0)
    for i in range(seqs_count):
        length = jnp.where(busy, own[i], other[i])
        long_seq = jnp.where(length == half, i, long_seq)
        long_start = jnp.where(length == half, busy_end, long_start)
        own_end, busy_end = own_end + own[i], busy_end + length
        own_ends.append(own_end)
        busy_ends.append(busy_end)
    return busy, light_total, long_seq, long_start, own_ends, busy_ends


def rest_rows(slot, light_total, long_start, half):
    rest = slot - light_total
    return rest, rest + jnp.where(rest >= long_start, half, 0)


def pack_kernel(seqs_count, lens_ref, hidden_ref, keep_ref, send_ref, pick_ref):
    rows_count = hidden_ref.shape[0]
    half = rows_count // 2
    busy, light_total, _, long_start, _, _ = row_plan(lens_ref, seqs_count, half)
    slot = lax.broadcasted_iota(jnp.int32, (half, rows_count), 0)
    row = lax.broadcasted_iota(jnp.int32, (half, rows_count), 1)
    rest, rest_row = rest_rows(slot, light_total, long_start, half)
    keep_src = jnp.where(busy, long_start + slot, jnp.where(rest < 0, slot, -1))
    send_src = jnp.where(busy & (rest >= 0), rest_row, -1)
    keep_pick = jnp.where(keep_src == row, 1.0, 0.0).astype(jnp.bfloat16)
    send_pick = jnp.where(send_src == row, 1.0, 0.0).astype(jnp.bfloat16)
    pick_ref[:half] = keep_pick
    pick_ref[half:] = send_pick
    hidden = hidden_ref[...]
    send_ref[...] = product(send_pick, hidden).astype(jnp.bfloat16)
    keep_ref[...] = product(keep_pick, hidden).astype(jnp.bfloat16)


def pack(resp_len, hidden, seqs_count):
    rows_count, shard = hidden.shape
    half = rows_count // 2
    vmem = pl.BlockSpec(memory_space=pltpu.VMEM)
    return pl.pallas_call(
        functools.partial(pack_kernel, seqs_count),
        out_shape=[
            jax.ShapeDtypeStruct((half, shard), jnp.bfloat16),
            jax.ShapeDtypeStruct((half, shard), jnp.bfloat16),
            jax.ShapeDtypeStruct((rows_count, rows_count), jnp.bfloat16),
        ],
        in_specs=[pl.BlockSpec(memory_space=pltpu.SMEM), vmem],
        out_specs=[vmem] * 3,
        compiler_params=pltpu.CompilerParams(vmem_limit_bytes=VMEM_LIMIT),
        name="pack_rows",
    )(resp_len, hidden)


def block_copies(ids, axis, own_ref, other_ref, held, sems):
    count = lax.axis_size("tensor")
    group = lax.axis_index("dp")
    size = own_ref.shape[axis] * 2 // count
    copies = []
    for j, block in enumerate(ids):
        place = pl.ds(pl.multiple_of((block % (count // 2)) * size, size), size)
        at = (place, slice(None)) if axis == 0 else (slice(None), place)
        here = pltpu.make_async_copy(own_ref.at[at], held.at[j], sems.at[j])
        there = pltpu.make_async_copy(other_ref.at[at], held.at[j], sems.at[j])
        copies.append((block // (count // 2) == group, here, there))
    return copies


def start_copies(copies):
    for is_here, here, there in copies:
        pl.when(is_here)(here.start)
        pl.when(jnp.logical_not(is_here))(there.start)


def query_blocks(blocks, shard, ids, copies, held, gain_ref, query, new_kv, squares):
    kv_head = lax.axis_index("tensor") * QH_DEV // GROUP
    kv_place = pl.ds(pl.multiple_of(shard + kv_head * 2 * HEAD, 2 * HEAD), 2 * HEAD)
    for j, block in enumerate(blocks):
        values = block[:, :shard].astype(jnp.float32)
        squares += jnp.sum(values * values, axis=1, keepdims=True)
        gained = (values * gain_ref[pl.ds(ids[j], 1), :]).astype(jnp.bfloat16)
        new_kv += block[:, kv_place].astype(jnp.float32)
        copies[j][1].wait()
        query += product(gained, held[j])
    return query, new_kv, squares


def query_kernel(shard, gain_ref, q_own, q_other, *refs):
    blocks, (query_ref, kv_ref, squares_ref, held, sems) = refs[:-5], refs[-5:]
    ids = gathered_ids()[: len(blocks)]
    copies = block_copies(ids, 0, q_own, q_other, held, sems)
    start_copies(copies)
    query, new_kv = jnp.zeros(query_ref.shape, jnp.float32), jnp.zeros(kv_ref.shape, jnp.float32)
    squares = jnp.zeros((query.shape[0], 1), jnp.float32)
    query, new_kv, squares = query_blocks(
        blocks, shard, ids, copies, held, gain_ref, query, new_kv, squares
    )
    query_ref[...] = query
    kv_ref[...] = new_kv
    squares_ref[...] = jnp.broadcast_to(squares, squares_ref.shape)


def query_part(gains, q_pair, blocks):
    shard, used, half = gains.shape[1], len(blocks), blocks[0].shape[0]
    q_width = q_pair[0].shape[1]
    vmem = pl.BlockSpec(memory_space=pltpu.VMEM)
    anywhere = pl.BlockSpec(memory_space=pltpu.HBM)
    return pl.pallas_call(
        functools.partial(query_kernel, shard),
        out_shape=[
            jax.ShapeDtypeStruct((half, q_width), jnp.float32),
            jax.ShapeDtypeStruct((half, 2 * HEAD), jnp.float32),
            jax.ShapeDtypeStruct((half, 128), jnp.float32),
        ],
        in_specs=[vmem] + [anywhere] * 2 + [vmem] * used,
        out_specs=[vmem] * 3,
        scratch_shapes=[
            pltpu.VMEM((used, shard, q_width), jnp.bfloat16),
            pltpu.SemaphoreType.DMA((used,)),
        ],
        compiler_params=pltpu.CompilerParams(vmem_limit_bytes=VMEM_LIMIT),
        cost_estimate=pl.CostEstimate(
            flops=2 * half * used * shard * q_width,
            bytes_accessed=2 * used * shard * (half + q_width),
            transcendentals=0,
        ),
        name="query_part",
    )(gains, *q_pair, *blocks)


def attention_kernel(
    seqs_count,
    lens_ref,
    ctx_ref,
    gain_ref,
    query_ref,
    kv_ref,
    squares_ref,
    block_ref,
    q_own,
    q_other,
    cache_own,
    cache_other,
    out_own,
    out_other,
    attn_ref,
    first_ref,
    q_held,
    cache_held,
    out_held,
    q_sems,
    cache_sems,
    out_sems,
):
    half, shard = first_ref.shape
    count = lax.axis_size("tensor")
    ctx_slots = cache_own.shape[1]
    ids = gathered_ids()[-1:]
    q_copies = block_copies(ids, 0, q_own, q_other, q_held, q_sems)
    out_copies = block_copies(scattered_ids()[1:2], 1, out_own, out_other, out_held, out_sems)
    cache_copies = [
        pltpu.make_async_copy(cache_own, cache_held.at[0], cache_sems.at[0]),
        pltpu.make_async_copy(cache_other, cache_held.at[1], cache_sems.at[1]),
    ]
    start_copies(q_copies)
    for copy in cache_copies:
        copy.start()
    start_copies(out_copies)

    query, new_kv, squares = query_blocks(
        [block_ref],
        shard,
        ids,
        q_copies,
        q_held,
        gain_ref,
        query_ref[...],
        kv_ref[...],
        squares_ref[:, :1],
    )
    scale = lax.rsqrt(squares / (shard * count) + EPS)
    query = (query * scale).astype(jnp.bfloat16)
    new_kv = (new_kv * scale).astype(jnp.bfloat16)

    busy, light_total, long_seq, long_start, own_ends, busy_ends = row_plan(
        lens_ref, seqs_count, half
    )

    def segments(slot):
        rest, rest_row = rest_rows(slot, light_total, long_start, half)
        own_seg, rest_seg = jnp.zeros_like(slot), jnp.full_like(slot, seqs_count)
        for i in range(seqs_count):
            own_seg += jnp.where(slot >= own_ends[i], 1, 0)
            rest_seg += jnp.where(rest_row >= busy_ends[i], 1, 0)
        return jnp.where(busy, long_seq, jnp.where(rest < 0, own_seg, rest_seg))

    slot = lax.broadcasted_iota(jnp.int32, (half, 1), 0)
    key_slot = lax.broadcasted_iota(jnp.int32, (1, half), 1)
    seg = segments(slot)
    own_ok = (segments(key_slot) == seg) & (key_slot <= slot)
    position = lax.broadcasted_iota(jnp.int32, (half, ctx_slots), 1)

    for copy in cache_copies:
        copy.wait()
    keys = cache_held[:, :, :, :HEAD].reshape(-1, HEAD)
    vals = cache_held[:, :, :, HEAD:].reshape(-1, HEAD)
    stacked = jnp.concatenate(
        [query[:, h * HEAD : (h + 1) * HEAD] for h in range(QH_DEV)], axis=0
    )
    contract = (((1,), (1,)), ((), ()))
    ctx_scores = lax.dot_general(stacked, keys, contract, preferred_element_type=jnp.float32)
    own_scores = lax.dot_general(
        stacked, new_kv[:, :HEAD], contract, preferred_element_type=jnp.float32
    )
    ctx_scores = ctx_scores * HEAD ** (-0.5)
    own_scores = own_scores * HEAD ** (-0.5)
    heads_ctx, heads_own = [], []
    for h in range(QH_DEV):
        rows = slice(h * half, (h + 1) * half)
        pieces = []
        for i in range(2 * seqs_count):
            allowed = (seg == i) & (position < ctx_ref[i])
            piece = ctx_scores[rows, i * ctx_slots : (i + 1) * ctx_slots]
            pieces.append(jnp.where(allowed, piece, -jnp.inf))
        scores = jnp.concatenate(pieces, axis=1)
        own = jnp.where(own_ok, own_scores[rows], -jnp.inf)
        top = jnp.maximum(
            jnp.max(scores, axis=1, keepdims=True), jnp.max(own, axis=1, keepdims=True)
        )
        weights, own_weights = jnp.exp(scores - top), jnp.exp(own - top)
        total = jnp.sum(weights, axis=1, keepdims=True) + jnp.sum(
            own_weights, axis=1, keepdims=True
        )
        heads_ctx.append((weights / total).astype(jnp.bfloat16))
        heads_own.append((own_weights / total).astype(jnp.bfloat16))
    mixed_vals = product(jnp.concatenate(heads_ctx, axis=0), vals) + product(
        jnp.concatenate(heads_own, axis=0), new_kv[:, HEAD:]
    )
    attn = jnp.concatenate(
        [mixed_vals[h * half : (h + 1) * half] for h in range(QH_DEV)], axis=1
    ).astype(jnp.bfloat16)
    attn_ref[...] = attn
    out_copies[0][1].wait()
    first_ref[...] = product(attn, out_held[0]).astype(jnp.bfloat16)


def attend(resp_len, both_ctx, gains, parts, block, q_pair, cache_pair, out_pair):
    half, shard = block.shape[0], gains.shape[1]
    seqs_count, ctx_slots, width = cache_pair[0].shape
    q_width, attn_width = q_pair[0].shape[1], out_pair[0].shape[0]
    vmem = pl.BlockSpec(memory_space=pltpu.VMEM)
    smem = pl.BlockSpec(memory_space=pltpu.SMEM)
    anywhere = pl.BlockSpec(memory_space=pltpu.HBM)
    return pl.pallas_call(
        functools.partial(attention_kernel, seqs_count),
        out_shape=[
            jax.ShapeDtypeStruct((half, attn_width), jnp.bfloat16),
            jax.ShapeDtypeStruct((half, shard), jnp.bfloat16),
        ],
        in_specs=[smem] * 2 + [vmem] * 5 + [anywhere] * 6,
        out_specs=[vmem] * 2,
        scratch_shapes=[
            pltpu.VMEM((1, shard, q_width), jnp.bfloat16),
            pltpu.VMEM((2, seqs_count, ctx_slots, width), jnp.bfloat16),
            pltpu.VMEM((1, attn_width, shard), jnp.bfloat16),
            pltpu.SemaphoreType.DMA((1,)),
            pltpu.SemaphoreType.DMA((2,)),
            pltpu.SemaphoreType.DMA((1,)),
        ],
        compiler_params=pltpu.CompilerParams(vmem_limit_bytes=VMEM_LIMIT),
        name="attend",
    )(resp_len, both_ctx, gains, *parts, block, *q_pair, *cache_pair, *out_pair)


def out_kernel(attn_ref, out_own, out_other, *refs):
    outs, (held, sems) = refs[:-2], refs[-2:]
    ids = scattered_ids()
    copies = block_copies(ids[:1] + ids[2:], 1, out_own, out_other, held, sems)
    start_copies(copies)
    attn = attn_ref[...]
    for j, out in enumerate(outs):
        copies[j][1].wait()
        out[...] = product(attn, held[j]).astype(jnp.bfloat16)


def out_products(attn, out_pair):
    half, attn_width = attn.shape
    count = lax.axis_size("tensor")
    shard = out_pair[0].shape[1] * 2 // count
    vmem = pl.BlockSpec(memory_space=pltpu.VMEM)
    anywhere = pl.BlockSpec(memory_space=pltpu.HBM)
    return pl.pallas_call(
        out_kernel,
        out_shape=[jax.ShapeDtypeStruct((half, shard), jnp.bfloat16)] * (count - 1),
        in_specs=[vmem] + [anywhere] * 2,
        out_specs=[vmem] * (count - 1),
        scratch_shapes=[
            pltpu.VMEM((count - 1, attn_width, shard), jnp.bfloat16),
            pltpu.SemaphoreType.DMA((count - 1,)),
        ],
        compiler_params=pltpu.CompilerParams(vmem_limit_bytes=VMEM_LIMIT),
        cost_estimate=pl.CostEstimate(
            flops=2 * half * (count - 1) * shard * attn_width,
            bytes_accessed=2 * (count - 1) * shard * (half + attn_width),
            transcendentals=0,
        ),
        name="out_products",
    )(attn, *out_pair)


def logit_blocks(blocks, ids, copies, held, gain_ref, logits, squares):
    for j, block in enumerate(blocks):
        values = block[...]
        mixed = values.astype(jnp.float32) / gain_ref[pl.ds(ids[j], 1), :]
        squares += jnp.sum(mixed * mixed, axis=1, keepdims=True)
        copies[j][1].wait()
        logits += product(values, held[j])
    return logits, squares


def logit_kernel(gain_ref, own_ref, other_ref, *refs):
    blocks, (logits_ref, squares_ref, held, sems) = refs[:-4], refs[-4:]
    ids = gathered_ids()[: len(blocks)]
    copies = block_copies(ids, 0, own_ref, other_ref, held, sems)
    start_copies(copies)
    logits = jnp.zeros(logits_ref.shape, jnp.float32)
    squares = jnp.zeros((logits.shape[0], 1), jnp.float32)
    logits, squares = logit_blocks(blocks, ids, copies, held, gain_ref, logits, squares)
    logits_ref[...] = logits
    squares_ref[...] = jnp.broadcast_to(squares, squares_ref.shape)


def logit_part(gains, vocab_pair, blocks):
    used, (half, shard) = len(blocks), blocks[0].shape
    vocab_count = vocab_pair[0].shape[1]
    vmem = pl.BlockSpec(memory_space=pltpu.VMEM)
    anywhere = pl.BlockSpec(memory_space=pltpu.HBM)
    return pl.pallas_call(
        logit_kernel,
        out_shape=[
            jax.ShapeDtypeStruct((half, vocab_count), jnp.float32),
            jax.ShapeDtypeStruct((half, 128), jnp.float32),
        ],
        in_specs=[vmem] + [anywhere] * 2 + [vmem] * used,
        out_specs=[vmem] * 2,
        scratch_shapes=[
            pltpu.VMEM((used, shard, vocab_count), jnp.bfloat16),
            pltpu.SemaphoreType.DMA((used,)),
        ],
        compiler_params=pltpu.CompilerParams(vmem_limit_bytes=VMEM_LIMIT),
        cost_estimate=pl.CostEstimate(
            flops=2 * half * used * shard * vocab_count,
            bytes_accessed=2 * used * shard * (half + vocab_count),
            transcendentals=0,
        ),
        name="logit_part",
    )(gains, *vocab_pair, *blocks)


def stats_kernel(
    targets_ref, gain_ref, logits_ref, squares_ref, block_ref, own_ref, other_ref, stats_ref, held, sems
):
    half, shard = block_ref.shape
    ids = gathered_ids()[-1:]
    copies = block_copies(ids, 0, own_ref, other_ref, held, sems)
    start_copies(copies)
    logits, squares = logit_blocks(
        [block_ref], ids, copies, held, gain_ref, logits_ref[...], squares_ref[:, :1]
    )
    logits = logits * lax.rsqrt(squares / (shard * lax.axis_size("tensor")) + EPS)
    vocab_count = logits.shape[1]
    column_ids = lax.axis_index("tensor") * vocab_count + lax.broadcasted_iota(
        jnp.int32, (half, vocab_count), 1
    )
    picked = jnp.sum(
        jnp.where(column_ids == targets_ref[...], logits, 0.0), axis=1, keepdims=True
    )
    top = jnp.max(logits, axis=1, keepdims=True)
    total = jnp.sum(jnp.exp(logits - top), axis=1, keepdims=True)
    lane = lax.broadcasted_iota(jnp.int32, (half, 128), 1)
    stats = jnp.where(lane == 0, top, jnp.where(lane == 1, total, picked))
    stats_ref[...] = jnp.transpose(stats)[:8]


def vocab_stats(targets, gains, parts, block, vocab_pair):
    half, shard = block.shape
    vocab_count = vocab_pair[0].shape[1]
    vmem = pl.BlockSpec(memory_space=pltpu.VMEM)
    anywhere = pl.BlockSpec(memory_space=pltpu.HBM)
    return pl.pallas_call(
        stats_kernel,
        out_shape=jax.ShapeDtypeStruct((8, half), jnp.float32),
        in_specs=[vmem] * 5 + [anywhere] * 2,
        out_specs=vmem,
        scratch_shapes=[
            pltpu.VMEM((1, shard, vocab_count), jnp.bfloat16),
            pltpu.SemaphoreType.DMA((1,)),
        ],
        compiler_params=pltpu.CompilerParams(vmem_limit_bytes=VMEM_LIMIT),
        name="vocab_stats",
    )(targets.reshape(half, 1), gains, *parts, block, *vocab_pair)


def per_device(
    hidden,
    attn_gain,
    q_weight,
    kv_weight,
    kv_cache,
    out_weight,
    final_gain,
    vocab_weight,
    resp_len,
    ctx_len,
    target_ids,
):
    rows_count, shard = hidden.shape
    half = rows_count // 2
    tensor_count = lax.axis_size("tensor")
    tensor_pos = lax.axis_index("tensor")
    group = lax.axis_index("dp")
    seqs_count = kv_cache.shape[0]

    keep, send, pick = pack(resp_len, hidden, seqs_count)
    rows = keep + swap_dp(send)
    rows_f = rows.astype(jnp.float32)

    gain = lax.dynamic_slice_in_dim(attn_gain, tensor_pos * shard, shard, 0)
    kv_partial = product((rows_f * gain).astype(jnp.bfloat16), kv_weight)
    cache = kv_cache
    if kv_cache.shape[2] != 2 * HEAD:
        kv_head = tensor_pos * QH_DEV // GROUP
        cache = lax.dynamic_slice_in_dim(kv_cache, kv_head * 2 * HEAD, 2 * HEAD, 2)
    def swap_rest(block):
        context = after(ctx_len, block)
        own_targets = lax.dynamic_slice_in_dim(
            after(target_ids, block), group * rows_count, rows_count, 0
        )
        sent_targets = jnp.sum(jnp.where(pick > 0, own_targets[None, :], 0), axis=1)
        return [
            swap_dp(after(cache, block)),
            jnp.concatenate([ctx_len, swap_dp(context)], axis=0),
            sent_targets[:half] + swap_dp(sent_targets[None, half:])[0],
        ]

    blocks, values = gather_blocks(
        jnp.concatenate([rows, kv_partial.astype(jnp.bfloat16)], axis=1),
        [
            lambda block: [swap_dp(after(q_weight, block))],
            lambda block: [swap_dp(after(out_weight, block))],
            swap_rest,
        ],
    )
    q_other, out_other, cache_other, both_ctx, targets = values
    q_pair, out_pair = (q_weight, q_other), (out_weight, out_other)
    gains = attn_gain.reshape(tensor_count, shard)
    parts = query_part(gains, q_pair, blocks[:-1])
    attn, first = attend(
        resp_len, both_ctx, gains, parts, blocks[-1], q_pair, (cache, cache_other), out_pair
    )
    products = out_products(attn, out_pair)
    products = [products[0], first, *products[1:]]

    partial = None
    for k in range(tensor_count // SIDE):
        total = products[2 * k].astype(jnp.float32) + swap_side(products[2 * k + 1]).astype(jnp.float32)
        if partial is not None:
            total = total + ring_step(partial).astype(jnp.float32)
        partial = total.astype(jnp.bfloat16)
    mixed = rows_f + total

    gain = lax.dynamic_slice_in_dim(final_gain, tensor_pos * shard, shard, 0)

    def place_rows(block):
        layer_rows = mixed.astype(jnp.bfloat16)
        layer_rows = jnp.concatenate([layer_rows, swap_dp(layer_rows)], axis=0)
        return [
            lax.dot_general(
                pick, layer_rows, (((0,), (0,)), ((), ())), preferred_element_type=jnp.float32
            ).astype(jnp.bfloat16)
        ]

    blocks, (layer_out, vocab_other) = gather_blocks(
        (mixed * gain).astype(jnp.bfloat16),
        [place_rows, lambda block: [swap_dp(after(vocab_weight, block))]],
    )
    gains = final_gain.reshape(tensor_count, shard)
    vocab_pair = (vocab_weight, vocab_other)
    parts = logit_part(gains, vocab_pair, blocks[:-1])
    stats = vocab_stats(targets, gains, parts, blocks[-1], vocab_pair)[:3]

    def join(parts):
        top = functools.reduce(jnp.maximum, [part[0] for part in parts])
        total = sum(part[1] * jnp.exp(part[0] - top) for part in parts)
        return jnp.stack([top, total, sum(part[2] for part in parts)])

    def in_order(part, others, place):
        held = [part, *others]
        return [
            functools.reduce(
                lambda a, c: jnp.where(place(c) == p, held[c], a), range(1, len(held)), held[0]
            )
            for p in range(len(held))
        ]

    side = tensor_pos % SIDE
    stats = join(in_order(stats, [swap_side(stats)], lambda c: side ^ c))
    ring_count = tensor_count // SIDE
    ring_pos = tensor_pos // SIDE
    others = [
        lax.ppermute(
            stats, "tensor", [(i, (i + SIDE * c) % tensor_count) for i in range(tensor_count)]
        )
        for c in range(1, ring_count)
    ]
    stats = join(
        in_order(stats, others, lambda c: (ring_pos - c + ring_count) % ring_count)
    )
    logprob = (stats[2] - stats[0] - jnp.log(stats[1]))[None, :]
    both_logprob = jnp.concatenate([logprob, swap_dp(logprob)], axis=1)
    token_logprob = jnp.sum(jnp.where(pick > 0, both_logprob.reshape(-1, 1), 0.0), axis=0)
    return (layer_out, token_logprob)


def solution(mesh):
    placed = (
        P(("rep", "dp"), "tensor"),
        P(),
        P("dp", "tensor"),
        P("tensor", None),
        P(("rep", "dp"), None, None),
        P("tensor", "dp"),
        P(),
        P("dp", "tensor"),
        P("rep"),
        P(("rep", "dp")),
        P("rep"),
    )
    return jax.shard_map(
        per_device,
        mesh=mesh,
        in_specs=placed,
        out_specs=(P(("rep", "dp"), "tensor"), P(("rep", "dp"))),
        check_vma=False,
    )
```

```python
import functools

import jax
import jax.numpy as jnp
from jax import lax
from jax.experimental import pallas as pl
from jax.experimental.pallas import tpu as pltpu
from jax.sharding import PartitionSpec as P

HEAD = 128
QH_DEV = 2
GROUP = 16
SIDE = 2
SWAP_STEP = {"q": 0, "out": 1, "cache": 1, "ctx": 2, "targets": 2, "layer": 5, "vocab": 5}


EPS = 1e-05
VMEM_LIMIT = 52 * 1024 * 1024


def product(left, right):
    return jnp.dot(left, right, preferred_element_type=jnp.float32)


def swap_dp(value):
    return lax.ppermute(value, "dp", [(0, 1), (1, 0)])


def swap_side(value):
    count = lax.axis_size("tensor")
    return lax.ppermute(value, "tensor", [(i, i ^ 1) for i in range(count)])


def ring_seat(seat, count):
    return jnp.where(seat == 0, 0, jnp.where(seat <= count // 2, 2 * seat - 1, 2 * (count - seat)))


def seat_of(place, count):
    return jnp.where(place % 2 == 1, (place + 1) // 2, (count - place // 2) % count)


def ring_step(value):
    count = lax.axis_size("tensor")
    ring = [0, *range(1, count // SIDE, 2), *range(count // SIDE - 2, 0, -2)]
    following = dict(zip(ring, ring[1:] + ring[:1]))
    pairs = [(i, following[i // SIDE] * SIDE + i % SIDE) for i in range(count)]
    return lax.ppermute(value, "tensor", pairs)


def after(value, *others):
    return lax.optimization_barrier((value, *others))[0]


def gather_blocks(block, beside=()):
    count = lax.axis_size("tensor") // SIDE
    blocks, values = [], []
    for k in range(count):
        crossed = swap_side(block)
        blocks += [block, crossed]
        ready = beside[k](block) if k < len(beside) else []
        values += ready
        if k + 1 < count:
            block = after(ring_step(block), crossed, *ready)
    return blocks, values


def ring_ids(first):
    count = lax.axis_size("tensor")
    pos = lax.axis_index("tensor")
    ring_count = count // SIDE
    seat = seat_of(pos // SIDE, ring_count)
    ids = []
    for k in range(first, first + ring_count):
        held = ring_seat((seat - k + 2 * ring_count) % ring_count, ring_count) * SIDE + pos % SIDE
        ids += [held, held ^ 1]
    return ids


def gathered_ids():
    return ring_ids(0)


def scattered_ids():
    return ring_ids(1)


def row_plan(lens_ref, seqs_count, half):
    group = lax.axis_index("dp")
    own = [lens_ref[group * seqs_count + i] for i in range(seqs_count)]
    other = [lens_ref[(1 - group) * seqs_count + i] for i in range(seqs_count)]
    busy = sum(own) > half
    light_total = jnp.where(busy, sum(other), sum(own))
    own_ends, busy_ends = [], []
    long_seq, long_start = jnp.int32(0), jnp.int32(0)
    own_end, busy_end = jnp.int32(0), jnp.int32(0)
    for i in range(seqs_count):
        length = jnp.where(busy, own[i], other[i])
        long_seq = jnp.where(length == half, i, long_seq)
        long_start = jnp.where(length == half, busy_end, long_start)
        own_end, busy_end = own_end + own[i], busy_end + length
        own_ends.append(own_end)
        busy_ends.append(busy_end)
    return busy, light_total, long_seq, long_start, own_ends, busy_ends


def rest_rows(slot, light_total, long_start, half):
    rest = slot - light_total
    return rest, rest + jnp.where(rest >= long_start, half, 0)


def pack_kernel(seqs_count, lens_ref, hidden_ref, keep_ref, send_ref, pick_ref):
    rows_count = hidden_ref.shape[0]
    half = rows_count // 2
    busy, light_total, _, long_start, _, _ = row_plan(lens_ref, seqs_count, half)
    slot = lax.broadcasted_iota(jnp.int32, (half, rows_count), 0)
    row = lax.broadcasted_iota(jnp.int32, (half, rows_count), 1)
    rest, rest_row = rest_rows(slot, light_total, long_start, half)
    keep_src = jnp.where(busy, long_start + slot, jnp.where(rest < 0, slot, -1))
    send_src = jnp.where(busy & (rest >= 0), rest_row, -1)
    keep_pick = jnp.where(keep_src == row, 1.0, 0.0).astype(jnp.bfloat16)
    send_pick = jnp.where(send_src == row, 1.0, 0.0).astype(jnp.bfloat16)
    pick_ref[:half] = keep_pick
    pick_ref[half:] = send_pick
    hidden = hidden_ref[...]
    send_ref[...] = product(send_pick, hidden).astype(jnp.bfloat16)
    keep_ref[...] = product(keep_pick, hidden).astype(jnp.bfloat16)


def pack(resp_len, hidden, seqs_count):
    rows_count, shard = hidden.shape
    half = rows_count // 2
    vmem = pl.BlockSpec(memory_space=pltpu.VMEM)
    return pl.pallas_call(
        functools.partial(pack_kernel, seqs_count),
        out_shape=[
            jax.ShapeDtypeStruct((half, shard), jnp.bfloat16),
            jax.ShapeDtypeStruct((half, shard), jnp.bfloat16),
            jax.ShapeDtypeStruct((rows_count, rows_count), jnp.bfloat16),
        ],
        in_specs=[pl.BlockSpec(memory_space=pltpu.SMEM), vmem],
        out_specs=[vmem] * 3,
        compiler_params=pltpu.CompilerParams(vmem_limit_bytes=VMEM_LIMIT),
        name="pack_rows",
    )(resp_len, hidden)


def block_copies(ids, axis, own_ref, other_ref, held, sems):
    count = lax.axis_size("tensor")
    group = lax.axis_index("dp")
    size = own_ref.shape[axis] * 2 // count
    copies = []
    places = held if isinstance(held, list) else [held.at[j] for j in range(len(ids))]
    for j, block in enumerate(ids):
        place = pl.ds(pl.multiple_of((block % (count // 2)) * size, size), size)
        at = (place, slice(None)) if axis == 0 else (slice(None), place)
        here = pltpu.make_async_copy(own_ref.at[at], places[j], sems.at[j])
        there = pltpu.make_async_copy(other_ref.at[at], places[j], sems.at[j])
        copies.append((block // (count // 2) == group, here, there))
    return copies


def start_copies(copies):
    for is_here, here, there in copies:
        pl.when(is_here)(here.start)
        pl.when(jnp.logical_not(is_here))(there.start)


def query_blocks(blocks, shard, ids, copies, held, gain_ref, query, new_kv, squares):
    kv_head = lax.axis_index("tensor") * QH_DEV // GROUP
    kv_place = pl.ds(pl.multiple_of(shard + kv_head * 2 * HEAD, 2 * HEAD), 2 * HEAD)
    for j, block in enumerate(blocks):
        values = block[:, :shard].astype(jnp.float32)
        squares += jnp.sum(values * values, axis=1, keepdims=True)
        gained = (values * gain_ref[pl.ds(ids[j], 1), :]).astype(jnp.bfloat16)
        new_kv += block[:, kv_place].astype(jnp.float32)
        copies[j][1].wait()
        query += product(gained, held[j])
    return query, new_kv, squares


def query_kernel(shard, gain_ref, q_own, q_other, *refs):
    blocks, (query_ref, kv_ref, squares_ref, held, sems) = refs[:-5], refs[-5:]
    ids = gathered_ids()[: len(blocks)]
    copies = block_copies(ids, 0, q_own, q_other, held, sems)
    start_copies(copies)
    query, new_kv = jnp.zeros(query_ref.shape, jnp.float32), jnp.zeros(kv_ref.shape, jnp.float32)
    squares = jnp.zeros((query.shape[0], 1), jnp.float32)
    query, new_kv, squares = query_blocks(
        blocks, shard, ids, copies, held, gain_ref, query, new_kv, squares
    )
    query_ref[...] = query
    kv_ref[...] = new_kv
    squares_ref[...] = jnp.broadcast_to(squares, squares_ref.shape)


def query_part(gains, q_pair, blocks):
    shard, used, half = gains.shape[1], len(blocks), blocks[0].shape[0]
    q_width = q_pair[0].shape[1]
    vmem = pl.BlockSpec(memory_space=pltpu.VMEM)
    anywhere = pl.BlockSpec(memory_space=pltpu.HBM)
    return pl.pallas_call(
        functools.partial(query_kernel, shard),
        out_shape=[
            jax.ShapeDtypeStruct((half, q_width), jnp.float32),
            jax.ShapeDtypeStruct((half, 2 * HEAD), jnp.float32),
            jax.ShapeDtypeStruct((half, 128), jnp.float32),
        ],
        in_specs=[vmem] + [anywhere] * 2 + [vmem] * used,
        out_specs=[vmem] * 3,
        scratch_shapes=[
            pltpu.VMEM((used, shard, q_width), jnp.bfloat16),
            pltpu.SemaphoreType.DMA((used,)),
        ],
        compiler_params=pltpu.CompilerParams(vmem_limit_bytes=VMEM_LIMIT),
        cost_estimate=pl.CostEstimate(
            flops=2 * half * used * shard * q_width,
            bytes_accessed=2 * used * shard * (half + q_width),
            transcendentals=0,
        ),
        name="query_part",
    )(gains, *q_pair, *blocks)


def attention_kernel(
    seqs_count,
    lens_ref,
    ctx_ref,
    gain_ref,
    query_ref,
    kv_ref,
    squares_ref,
    block_ref,
    q_own,
    q_other,
    cache_own,
    cache_other,
    out_own,
    out_other,
    attn_ref,
    first_ref,
    q_held,
    cache_held,
    out_held,
    q_sems,
    cache_sems,
    out_sems,
):
    half, shard = first_ref.shape
    count = lax.axis_size("tensor")
    ctx_slots = cache_own.shape[1]
    ids = gathered_ids()[-1:]
    q_copies = block_copies(ids, 0, q_own, q_other, q_held, q_sems)
    out_copies = block_copies(scattered_ids()[1:2], 1, out_own, out_other, out_held, out_sems)
    cache_copies = [
        pltpu.make_async_copy(cache_own, cache_held.at[0], cache_sems.at[0]),
        pltpu.make_async_copy(cache_other, cache_held.at[1], cache_sems.at[1]),
    ]
    start_copies(q_copies)
    for copy in cache_copies:
        copy.start()
    start_copies(out_copies)

    query, new_kv, squares = query_blocks(
        [block_ref],
        shard,
        ids,
        q_copies,
        q_held,
        gain_ref,
        query_ref[...],
        kv_ref[...],
        squares_ref[:, :1],
    )
    scale = lax.rsqrt(squares / (shard * count) + EPS)
    query = (query * scale).astype(jnp.bfloat16)
    new_kv = (new_kv * scale).astype(jnp.bfloat16)

    busy, light_total, long_seq, long_start, own_ends, busy_ends = row_plan(
        lens_ref, seqs_count, half
    )

    def segments(slot):
        rest, rest_row = rest_rows(slot, light_total, long_start, half)
        own_seg, rest_seg = jnp.zeros_like(slot), jnp.full_like(slot, seqs_count)
        for i in range(seqs_count):
            own_seg += jnp.where(slot >= own_ends[i], 1, 0)
            rest_seg += jnp.where(rest_row >= busy_ends[i], 1, 0)
        return jnp.where(busy, long_seq, jnp.where(rest < 0, own_seg, rest_seg))

    slot = lax.broadcasted_iota(jnp.int32, (half, 1), 0)
    key_slot = lax.broadcasted_iota(jnp.int32, (1, half), 1)
    seg = segments(slot)
    own_ok = (segments(key_slot) == seg) & (key_slot <= slot)
    position = lax.broadcasted_iota(jnp.int32, (half, ctx_slots), 1)

    for copy in cache_copies:
        copy.wait()
    keys = cache_held[:, :, :, :HEAD].reshape(-1, HEAD)
    vals = cache_held[:, :, :, HEAD:].reshape(-1, HEAD)
    stacked = jnp.concatenate(
        [query[:, h * HEAD : (h + 1) * HEAD] for h in range(QH_DEV)], axis=0
    )
    contract = (((1,), (1,)), ((), ()))
    ctx_scores = lax.dot_general(stacked, keys, contract, preferred_element_type=jnp.float32)
    own_scores = lax.dot_general(
        stacked, new_kv[:, :HEAD], contract, preferred_element_type=jnp.float32
    )
    ctx_scores = ctx_scores * HEAD ** (-0.5)
    own_scores = own_scores * HEAD ** (-0.5)
    heads_ctx, heads_own = [], []
    for h in range(QH_DEV):
        rows = slice(h * half, (h + 1) * half)
        pieces = []
        for i in range(2 * seqs_count):
            allowed = (seg == i) & (position < ctx_ref[i])
            piece = ctx_scores[rows, i * ctx_slots : (i + 1) * ctx_slots]
            pieces.append(jnp.where(allowed, piece, -jnp.inf))
        scores = jnp.concatenate(pieces, axis=1)
        own = jnp.where(own_ok, own_scores[rows], -jnp.inf)
        top = jnp.maximum(
            jnp.max(scores, axis=1, keepdims=True), jnp.max(own, axis=1, keepdims=True)
        )
        weights, own_weights = jnp.exp(scores - top), jnp.exp(own - top)
        total = jnp.sum(weights, axis=1, keepdims=True) + jnp.sum(
            own_weights, axis=1, keepdims=True
        )
        heads_ctx.append((weights / total).astype(jnp.bfloat16))
        heads_own.append((own_weights / total).astype(jnp.bfloat16))
    mixed_vals = product(jnp.concatenate(heads_ctx, axis=0), vals) + product(
        jnp.concatenate(heads_own, axis=0), new_kv[:, HEAD:]
    )
    attn = jnp.concatenate(
        [mixed_vals[h * half : (h + 1) * half] for h in range(QH_DEV)], axis=1
    ).astype(jnp.bfloat16)
    attn_ref[...] = attn
    out_copies[0][1].wait()
    first_ref[...] = product(attn, out_held[0]).astype(jnp.bfloat16)


def attend(resp_len, both_ctx, gains, parts, block, q_pair, cache_pair, out_pair):
    half, shard = block.shape[0], gains.shape[1]
    seqs_count, ctx_slots, width = cache_pair[0].shape
    q_width, attn_width = q_pair[0].shape[1], out_pair[0].shape[0]
    vmem = pl.BlockSpec(memory_space=pltpu.VMEM)
    smem = pl.BlockSpec(memory_space=pltpu.SMEM)
    anywhere = pl.BlockSpec(memory_space=pltpu.HBM)
    return pl.pallas_call(
        functools.partial(attention_kernel, seqs_count),
        out_shape=[
            jax.ShapeDtypeStruct((half, attn_width), jnp.bfloat16),
            jax.ShapeDtypeStruct((half, shard), jnp.bfloat16),
        ],
        in_specs=[smem] * 2 + [vmem] * 5 + [anywhere] * 6,
        out_specs=[vmem] * 2,
        scratch_shapes=[
            pltpu.VMEM((1, shard, q_width), jnp.bfloat16),
            pltpu.VMEM((2, seqs_count, ctx_slots, width), jnp.bfloat16),
            pltpu.VMEM((1, attn_width, shard), jnp.bfloat16),
            pltpu.SemaphoreType.DMA((1,)),
            pltpu.SemaphoreType.DMA((2,)),
            pltpu.SemaphoreType.DMA((1,)),
        ],
        compiler_params=pltpu.CompilerParams(vmem_limit_bytes=VMEM_LIMIT),
        name="attend",
    )(resp_len, both_ctx, gains, *parts, block, *q_pair, *cache_pair, *out_pair)


def out_kernel(attn_ref, out_own, out_other, *refs):
    outs, (held, sems) = refs[:-2], refs[-2:]
    ids = scattered_ids()
    copies = block_copies(ids[:1] + ids[2:], 1, out_own, out_other, held, sems)
    start_copies(copies)
    attn = attn_ref[...]
    for j, out in enumerate(outs):
        copies[j][1].wait()
        out[...] = product(attn, held[j]).astype(jnp.bfloat16)


def out_products(attn, out_pair):
    half, attn_width = attn.shape
    count = lax.axis_size("tensor")
    shard = out_pair[0].shape[1] * 2 // count
    vmem = pl.BlockSpec(memory_space=pltpu.VMEM)
    anywhere = pl.BlockSpec(memory_space=pltpu.HBM)
    return pl.pallas_call(
        out_kernel,
        out_shape=[jax.ShapeDtypeStruct((half, shard), jnp.bfloat16)] * (count - 1),
        in_specs=[vmem] + [anywhere] * 2,
        out_specs=[vmem] * (count - 1),
        scratch_shapes=[
            pltpu.VMEM((count - 1, attn_width, shard), jnp.bfloat16),
            pltpu.SemaphoreType.DMA((count - 1,)),
        ],
        compiler_params=pltpu.CompilerParams(vmem_limit_bytes=VMEM_LIMIT),
        cost_estimate=pl.CostEstimate(
            flops=2 * half * (count - 1) * shard * attn_width,
            bytes_accessed=2 * (count - 1) * shard * (half + attn_width),
            transcendentals=0,
        ),
        name="out_products",
    )(attn, *out_pair)


def logit_blocks(blocks, ids, copies, held, gain_ref, logits, squares):
    for j, block in enumerate(blocks):
        values = block[...]
        mixed = values.astype(jnp.float32) / gain_ref[pl.ds(ids[j], 1), :]
        squares += jnp.sum(mixed * mixed, axis=1, keepdims=True)
        copies[j][1].wait()
        logits += product(values, held[j])
    return logits, squares


def logit_kernel(gain_ref, own_ref, other_ref, *refs):
    blocks, (logits_ref, squares_ref, held, sems) = refs[:-4], refs[-4:]
    ids = gathered_ids()[: len(blocks)]
    copies = block_copies(ids, 0, own_ref, other_ref, held, sems)
    start_copies(copies)
    logits = jnp.zeros(logits_ref.shape, jnp.float32)
    squares = jnp.zeros((logits.shape[0], 1), jnp.float32)
    logits, squares = logit_blocks(blocks, ids, copies, held, gain_ref, logits, squares)
    logits_ref[...] = logits
    squares_ref[...] = jnp.broadcast_to(squares, squares_ref.shape)


def logit_part(gains, vocab_pair, blocks):
    used, (half, shard) = len(blocks), blocks[0].shape
    vocab_count = vocab_pair[0].shape[1]
    vmem = pl.BlockSpec(memory_space=pltpu.VMEM)
    anywhere = pl.BlockSpec(memory_space=pltpu.HBM)
    return pl.pallas_call(
        logit_kernel,
        out_shape=[
            jax.ShapeDtypeStruct((half, vocab_count), jnp.float32),
            jax.ShapeDtypeStruct((half, 128), jnp.float32),
        ],
        in_specs=[vmem] + [anywhere] * 2 + [vmem] * used,
        out_specs=[vmem] * 2,
        scratch_shapes=[
            pltpu.VMEM((used, shard, vocab_count), jnp.bfloat16),
            pltpu.SemaphoreType.DMA((used,)),
        ],
        compiler_params=pltpu.CompilerParams(vmem_limit_bytes=VMEM_LIMIT),
        cost_estimate=pl.CostEstimate(
            flops=2 * half * used * shard * vocab_count,
            bytes_accessed=2 * used * shard * (half + vocab_count),
            transcendentals=0,
        ),
        name="logit_part",
    )(gains, *vocab_pair, *blocks)


def stats_kernel(
    targets_ref, gain_ref, logits_ref, squares_ref, block_ref, own_ref, other_ref, stats_ref, held, sems
):
    half, shard = block_ref.shape
    ids = gathered_ids()[-1:]
    copies = block_copies(ids, 0, own_ref, other_ref, held, sems)
    start_copies(copies)
    logits, squares = logit_blocks(
        [block_ref], ids, copies, held, gain_ref, logits_ref[...], squares_ref[:, :1]
    )
    logits = logits * lax.rsqrt(squares / (shard * lax.axis_size("tensor")) + EPS)
    vocab_count = logits.shape[1]
    column_ids = lax.axis_index("tensor") * vocab_count + lax.broadcasted_iota(
        jnp.int32, (half, vocab_count), 1
    )
    picked = jnp.sum(
        jnp.where(column_ids == targets_ref[...], logits, 0.0), axis=1, keepdims=True
    )
    top = jnp.max(logits, axis=1, keepdims=True)
    total = jnp.sum(jnp.exp(logits - top), axis=1, keepdims=True)
    lane = lax.broadcasted_iota(jnp.int32, (half, 128), 1)
    stats = jnp.where(lane == 0, top, jnp.where(lane == 1, total, picked))
    stats_ref[...] = jnp.transpose(stats)[:8]


def vocab_stats(targets, gains, parts, block, vocab_pair):
    half, shard = block.shape
    vocab_count = vocab_pair[0].shape[1]
    vmem = pl.BlockSpec(memory_space=pltpu.VMEM)
    anywhere = pl.BlockSpec(memory_space=pltpu.HBM)
    return pl.pallas_call(
        stats_kernel,
        out_shape=jax.ShapeDtypeStruct((8, half), jnp.float32),
        in_specs=[vmem] * 5 + [anywhere] * 2,
        out_specs=vmem,
        scratch_shapes=[
            pltpu.VMEM((1, shard, vocab_count), jnp.bfloat16),
            pltpu.SemaphoreType.DMA((1,)),
        ],
        compiler_params=pltpu.CompilerParams(vmem_limit_bytes=VMEM_LIMIT),
        name="vocab_stats",
    )(targets.reshape(half, 1), gains, *parts, block, *vocab_pair)


def per_device(
    hidden,
    attn_gain,
    q_weight,
    kv_weight,
    kv_cache,
    out_weight,
    final_gain,
    vocab_weight,
    resp_len,
    ctx_len,
    target_ids,
):
    rows_count, shard = hidden.shape
    half = rows_count // 2
    tensor_count = lax.axis_size("tensor")
    tensor_pos = lax.axis_index("tensor")
    group = lax.axis_index("dp")
    seqs_count = kv_cache.shape[0]

    keep, send, pick = pack(resp_len, hidden, seqs_count)
    rows = keep + swap_dp(send)
    rows_f = rows.astype(jnp.float32)

    gain = lax.dynamic_slice_in_dim(attn_gain, tensor_pos * shard, shard, 0)
    kv_partial = product((rows_f * gain).astype(jnp.bfloat16), kv_weight)
    cache = kv_cache
    if kv_cache.shape[2] != 2 * HEAD:
        kv_head = tensor_pos * QH_DEV // GROUP
        cache = lax.dynamic_slice_in_dim(kv_cache, kv_head * 2 * HEAD, 2 * HEAD, 2)
    moved = {}

    def swap_rows(value):
        return lambda block: swap_dp(after(value, block))

    def swap_targets(block):
        own_targets = lax.dynamic_slice_in_dim(
            after(target_ids, block), group * rows_count, rows_count, 0
        )
        sent_targets = jnp.sum(jnp.where(pick > 0, own_targets[None, :], 0), axis=1)
        return sent_targets[:half] + swap_dp(sent_targets[None, half:])[0]

    moves = {
        "q": swap_rows(q_weight),
        "out": swap_rows(out_weight),
        "cache": swap_rows(cache),
        "ctx": lambda block: jnp.concatenate([ctx_len, swap_dp(after(ctx_len, block))], axis=0),
        "targets": swap_targets,
        "vocab": swap_rows(vocab_weight),
    }

    def moves_at(step):
        def run(block):
            for name in moves:
                if SWAP_STEP[name] == step:
                    moved[name] = moves[name](block)
            return [moved[name] for name in moves if SWAP_STEP[name] == step]

        return run

    blocks, _ = gather_blocks(
        jnp.concatenate([rows, kv_partial.astype(jnp.bfloat16)], axis=1),
        [moves_at(step) for step in range(4)],
    )
    q_other, out_other, cache_other = moved["q"], moved["out"], moved["cache"]
    both_ctx = moved["ctx"]
    q_pair, out_pair = (q_weight, q_other), (out_weight, out_other)
    gains = attn_gain.reshape(tensor_count, shard)
    parts = query_part(gains, q_pair, blocks[:-1])
    attn, first = attend(
        resp_len, both_ctx, gains, parts, blocks[-1], q_pair, (cache, cache_other), out_pair
    )
    products = out_products(attn, out_pair)
    products = [products[0], first, *products[1:]]

    partial = None
    for k in range(tensor_count // SIDE):
        total = products[2 * k].astype(jnp.float32) + swap_side(products[2 * k + 1]).astype(jnp.float32)
        if partial is not None:
            total = total + ring_step(partial).astype(jnp.float32)
        partial = total.astype(jnp.bfloat16)
    mixed = rows_f + total

    gain = lax.dynamic_slice_in_dim(final_gain, tensor_pos * shard, shard, 0)

    def place_rows(block):
        layer_rows = mixed.astype(jnp.bfloat16)
        if SWAP_STEP["layer"] > 4:
            layer_rows = after(layer_rows, block)
        layer_rows = jnp.concatenate([layer_rows, swap_dp(layer_rows)], axis=0)
        return lax.dot_general(
            pick, layer_rows, (((0,), (0,)), ((), ())), preferred_element_type=jnp.float32
        ).astype(jnp.bfloat16)

    moves["layer"] = place_rows
    blocks, _ = gather_blocks(
        (mixed * gain).astype(jnp.bfloat16), [moves_at(step) for step in range(4, 8)]
    )
    layer_out, vocab_other, targets = moved["layer"], moved["vocab"], moved["targets"]
    gains = final_gain.reshape(tensor_count, shard)
    vocab_pair = (vocab_weight, vocab_other)
    parts = logit_part(gains, vocab_pair, blocks[:-1])
    stats = vocab_stats(targets, gains, parts, blocks[-1], vocab_pair)[:3]

    def join(parts):
        top = functools.reduce(jnp.maximum, [part[0] for part in parts])
        total = sum(part[1] * jnp.exp(part[0] - top) for part in parts)
        return jnp.stack([top, total, sum(part[2] for part in parts)])

    def in_order(part, others, place):
        held = [part, *others]
        return [
            functools.reduce(
                lambda a, c: jnp.where(place(c) == p, held[c], a), range(1, len(held)), held[0]
            )
            for p in range(len(held))
        ]

    side = tensor_pos % SIDE
    stats = join(in_order(stats, [swap_side(stats)], lambda c: side ^ c))
    ring_count = tensor_count // SIDE
    ring_pos = tensor_pos // SIDE
    others = [
        lax.ppermute(
            stats, "tensor", [(i, (i + SIDE * c) % tensor_count) for i in range(tensor_count)]
        )
        for c in range(1, ring_count)
    ]
    stats = join(
        in_order(stats, others, lambda c: (ring_pos - c + ring_count) % ring_count)
    )
    logprob = (stats[2] - stats[0] - jnp.log(stats[1]))[None, :]
    both_logprob = jnp.concatenate([logprob, swap_dp(logprob)], axis=1)
    token_logprob = jnp.sum(jnp.where(pick > 0, both_logprob.reshape(-1, 1), 0.0), axis=0)
    return (layer_out, token_logprob)


def solution(mesh):
    placed = (
        P(("rep", "dp"), "tensor"),
        P(),
        P("dp", "tensor"),
        P("tensor", None),
        P(("rep", "dp"), None, None),
        P("tensor", "dp"),
        P(),
        P("dp", "tensor"),
        P("rep"),
        P(("rep", "dp")),
        P("rep"),
    )
    return jax.shard_map(
        per_device,
        mesh=mesh,
        in_specs=placed,
        out_specs=(P(("rep", "dp"), "tensor"), P(("rep", "dp"))),
        check_vma=False,
    )
```

```python
import functools

import jax
import jax.numpy as jnp
from jax import lax
from jax.experimental import pallas as pl
from jax.experimental.pallas import tpu as pltpu
from jax.sharding import PartitionSpec as P

HEAD = 128
QH_DEV = 2
GROUP = 16
SIDE = 2
SWAP_STEP = {"q": 0, "out": 0, "cache": 1, "ctx": 2, "targets": 2, "layer": 5, "vocab": 5}


EPS = 1e-05
VMEM_LIMIT = 52 * 1024 * 1024


def product(left, right):
    return jnp.dot(left, right, preferred_element_type=jnp.float32)


def swap_dp(value):
    return lax.ppermute(value, "dp", [(0, 1), (1, 0)])


def swap_side(value):
    count = lax.axis_size("tensor")
    return lax.ppermute(value, "tensor", [(i, i ^ 1) for i in range(count)])


def ring_seat(seat, count):
    return jnp.where(seat == 0, 0, jnp.where(seat <= count // 2, 2 * seat - 1, 2 * (count - seat)))


def seat_of(place, count):
    return jnp.where(place % 2 == 1, (place + 1) // 2, (count - place // 2) % count)


def ring_step(value):
    count = lax.axis_size("tensor")
    ring = [0, *range(1, count // SIDE, 2), *range(count // SIDE - 2, 0, -2)]
    following = dict(zip(ring, ring[1:] + ring[:1]))
    pairs = [(i, following[i // SIDE] * SIDE + i % SIDE) for i in range(count)]
    return lax.ppermute(value, "tensor", pairs)


def after(value, *others):
    return lax.optimization_barrier((value, *others))[0]


def gather_blocks(block, beside=()):
    count = lax.axis_size("tensor") // SIDE
    blocks, values = [], []
    for k in range(count):
        crossed = swap_side(block)
        blocks += [block, crossed]
        ready = beside[k](block) if k < len(beside) else []
        values += ready
        if k + 1 < count:
            block = after(ring_step(block), crossed, *ready)
    return blocks, values


def ring_ids(first):
    count = lax.axis_size("tensor")
    pos = lax.axis_index("tensor")
    ring_count = count // SIDE
    seat = seat_of(pos // SIDE, ring_count)
    ids = []
    for k in range(first, first + ring_count):
        held = ring_seat((seat - k + 2 * ring_count) % ring_count, ring_count) * SIDE + pos % SIDE
        ids += [held, held ^ 1]
    return ids


def gathered_ids():
    return ring_ids(0)


def scattered_ids():
    return ring_ids(1)


def row_plan(lens_ref, seqs_count, half):
    group = lax.axis_index("dp")
    own = [lens_ref[group * seqs_count + i] for i in range(seqs_count)]
    other = [lens_ref[(1 - group) * seqs_count + i] for i in range(seqs_count)]
    busy = sum(own) > half
    light_total = jnp.where(busy, sum(other), sum(own))
    own_ends, busy_ends = [], []
    long_seq, long_start = jnp.int32(0), jnp.int32(0)
    own_end, busy_end = jnp.int32(0), jnp.int32(0)
    for i in range(seqs_count):
        length = jnp.where(busy, own[i], other[i])
        long_seq = jnp.where(length == half, i, long_seq)
        long_start = jnp.where(length == half, busy_end, long_start)
        own_end, busy_end = own_end + own[i], busy_end + length
        own_ends.append(own_end)
        busy_ends.append(busy_end)
    return busy, light_total, long_seq, long_start, own_ends, busy_ends


def rest_rows(slot, light_total, long_start, half):
    rest = slot - light_total
    return rest, rest + jnp.where(rest >= long_start, half, 0)


def pack_kernel(seqs_count, lens_ref, hidden_ref, keep_ref, send_ref, pick_ref):
    rows_count = hidden_ref.shape[0]
    half = rows_count // 2
    busy, light_total, _, long_start, _, _ = row_plan(lens_ref, seqs_count, half)
    slot = lax.broadcasted_iota(jnp.int32, (half, rows_count), 0)
    row = lax.broadcasted_iota(jnp.int32, (half, rows_count), 1)
    rest, rest_row = rest_rows(slot, light_total, long_start, half)
    keep_src = jnp.where(busy, long_start + slot, jnp.where(rest < 0, slot, -1))
    send_src = jnp.where(busy & (rest >= 0), rest_row, -1)
    keep_pick = jnp.where(keep_src == row, 1.0, 0.0).astype(jnp.bfloat16)
    send_pick = jnp.where(send_src == row, 1.0, 0.0).astype(jnp.bfloat16)
    pick_ref[:half] = keep_pick
    pick_ref[half:] = send_pick
    hidden = hidden_ref[...]
    send_ref[...] = product(send_pick, hidden).astype(jnp.bfloat16)
    keep_ref[...] = product(keep_pick, hidden).astype(jnp.bfloat16)


def pack(resp_len, hidden, seqs_count):
    rows_count, shard = hidden.shape
    half = rows_count // 2
    vmem = pl.BlockSpec(memory_space=pltpu.VMEM)
    return pl.pallas_call(
        functools.partial(pack_kernel, seqs_count),
        out_shape=[
            jax.ShapeDtypeStruct((half, shard), jnp.bfloat16),
            jax.ShapeDtypeStruct((half, shard), jnp.bfloat16),
            jax.ShapeDtypeStruct((rows_count, rows_count), jnp.bfloat16),
        ],
        in_specs=[pl.BlockSpec(memory_space=pltpu.SMEM), vmem],
        out_specs=[vmem] * 3,
        compiler_params=pltpu.CompilerParams(vmem_limit_bytes=VMEM_LIMIT),
        name="pack_rows",
    )(resp_len, hidden)


def block_copies(ids, axis, own_ref, other_ref, held, sems):
    count = lax.axis_size("tensor")
    group = lax.axis_index("dp")
    size = own_ref.shape[axis] * 2 // count
    copies = []
    places = held if isinstance(held, list) else [held.at[j] for j in range(len(ids))]
    for j, block in enumerate(ids):
        place = pl.ds(pl.multiple_of((block % (count // 2)) * size, size), size)
        at = (place, slice(None)) if axis == 0 else (slice(None), place)
        here = pltpu.make_async_copy(own_ref.at[at], places[j], sems.at[j])
        there = pltpu.make_async_copy(other_ref.at[at], places[j], sems.at[j])
        copies.append((block // (count // 2) == group, here, there))
    return copies


def start_copies(copies):
    for is_here, here, there in copies:
        pl.when(is_here)(here.start)
        pl.when(jnp.logical_not(is_here))(there.start)


def query_blocks(blocks, shard, ids, copies, held, gain_ref, query, new_kv, squares):
    kv_head = lax.axis_index("tensor") * QH_DEV // GROUP
    kv_place = pl.ds(pl.multiple_of(shard + kv_head * 2 * HEAD, 2 * HEAD), 2 * HEAD)
    for j, block in enumerate(blocks):
        values = block[:, :shard].astype(jnp.float32)
        squares += jnp.sum(values * values, axis=1, keepdims=True)
        gained = (values * gain_ref[pl.ds(ids[j], 1), :]).astype(jnp.bfloat16)
        new_kv += block[:, kv_place].astype(jnp.float32)
        copies[j][1].wait()
        query += product(gained, held[j])
    return query, new_kv, squares


def query_kernel(shard, gain_ref, q_own, q_other, *refs):
    blocks, (query_ref, kv_ref, squares_ref, held, sems) = refs[:-5], refs[-5:]
    ids = gathered_ids()[: len(blocks)]
    copies = block_copies(ids, 0, q_own, q_other, held, sems)
    start_copies(copies)
    query, new_kv = jnp.zeros(query_ref.shape, jnp.float32), jnp.zeros(kv_ref.shape, jnp.float32)
    squares = jnp.zeros((query.shape[0], 1), jnp.float32)
    query, new_kv, squares = query_blocks(
        blocks, shard, ids, copies, held, gain_ref, query, new_kv, squares
    )
    query_ref[...] = query
    kv_ref[...] = new_kv
    squares_ref[...] = jnp.broadcast_to(squares, squares_ref.shape)


def query_part(gains, q_pair, blocks):
    shard, used, half = gains.shape[1], len(blocks), blocks[0].shape[0]
    q_width = q_pair[0].shape[1]
    vmem = pl.BlockSpec(memory_space=pltpu.VMEM)
    anywhere = pl.BlockSpec(memory_space=pltpu.HBM)
    return pl.pallas_call(
        functools.partial(query_kernel, shard),
        out_shape=[
            jax.ShapeDtypeStruct((half, q_width), jnp.float32),
            jax.ShapeDtypeStruct((half, 2 * HEAD), jnp.float32),
            jax.ShapeDtypeStruct((half, 128), jnp.float32),
        ],
        in_specs=[vmem] + [anywhere] * 2 + [vmem] * used,
        out_specs=[vmem] * 3,
        scratch_shapes=[
            pltpu.VMEM((used, shard, q_width), jnp.bfloat16),
            pltpu.SemaphoreType.DMA((used,)),
        ],
        compiler_params=pltpu.CompilerParams(vmem_limit_bytes=VMEM_LIMIT),
        cost_estimate=pl.CostEstimate(
            flops=2 * half * used * shard * q_width,
            bytes_accessed=2 * used * shard * (half + q_width),
            transcendentals=0,
        ),
        name="query_part",
    )(gains, *q_pair, *blocks)


def attention_kernel(
    seqs_count,
    lens_ref,
    ctx_ref,
    gain_ref,
    query_ref,
    kv_ref,
    squares_ref,
    block_ref,
    q_own,
    q_other,
    cache_own,
    cache_other,
    out_own,
    out_other,
    attn_ref,
    first_ref,
    q_held,
    cache_held,
    out_held,
    q_sems,
    cache_sems,
    out_sems,
):
    half, shard = first_ref.shape
    count = lax.axis_size("tensor")
    ctx_slots = cache_own.shape[1]
    ids = gathered_ids()[-1:]
    q_copies = block_copies(ids, 0, q_own, q_other, q_held, q_sems)
    out_copies = block_copies(scattered_ids()[1:2], 1, out_own, out_other, out_held, out_sems)
    cache_copies = [
        pltpu.make_async_copy(cache_own, cache_held.at[0], cache_sems.at[0]),
        pltpu.make_async_copy(cache_other, cache_held.at[1], cache_sems.at[1]),
    ]
    start_copies(q_copies)
    for copy in cache_copies:
        copy.start()
    start_copies(out_copies)

    query, new_kv, squares = query_blocks(
        [block_ref],
        shard,
        ids,
        q_copies,
        q_held,
        gain_ref,
        query_ref[...],
        kv_ref[...],
        squares_ref[:, :1],
    )
    scale = lax.rsqrt(squares / (shard * count) + EPS)
    query = (query * scale).astype(jnp.bfloat16)
    new_kv = (new_kv * scale).astype(jnp.bfloat16)

    busy, light_total, long_seq, long_start, own_ends, busy_ends = row_plan(
        lens_ref, seqs_count, half
    )

    def segments(slot):
        rest, rest_row = rest_rows(slot, light_total, long_start, half)
        own_seg, rest_seg = jnp.zeros_like(slot), jnp.full_like(slot, seqs_count)
        for i in range(seqs_count):
            own_seg += jnp.where(slot >= own_ends[i], 1, 0)
            rest_seg += jnp.where(rest_row >= busy_ends[i], 1, 0)
        return jnp.where(busy, long_seq, jnp.where(rest < 0, own_seg, rest_seg))

    slot = lax.broadcasted_iota(jnp.int32, (half, 1), 0)
    key_slot = lax.broadcasted_iota(jnp.int32, (1, half), 1)
    seg = segments(slot)
    own_ok = (segments(key_slot) == seg) & (key_slot <= slot)
    position = lax.broadcasted_iota(jnp.int32, (half, ctx_slots), 1)

    for copy in cache_copies:
        copy.wait()
    keys = cache_held[:, :, :, :HEAD].reshape(-1, HEAD)
    vals = cache_held[:, :, :, HEAD:].reshape(-1, HEAD)
    stacked = jnp.concatenate(
        [query[:, h * HEAD : (h + 1) * HEAD] for h in range(QH_DEV)], axis=0
    )
    contract = (((1,), (1,)), ((), ()))
    ctx_scores = lax.dot_general(stacked, keys, contract, preferred_element_type=jnp.float32)
    own_scores = lax.dot_general(
        stacked, new_kv[:, :HEAD], contract, preferred_element_type=jnp.float32
    )
    ctx_scores = ctx_scores * HEAD ** (-0.5)
    own_scores = own_scores * HEAD ** (-0.5)
    heads_ctx, heads_own = [], []
    for h in range(QH_DEV):
        rows = slice(h * half, (h + 1) * half)
        pieces = []
        for i in range(2 * seqs_count):
            allowed = (seg == i) & (position < ctx_ref[i])
            piece = ctx_scores[rows, i * ctx_slots : (i + 1) * ctx_slots]
            pieces.append(jnp.where(allowed, piece, -jnp.inf))
        scores = jnp.concatenate(pieces, axis=1)
        own = jnp.where(own_ok, own_scores[rows], -jnp.inf)
        top = jnp.maximum(
            jnp.max(scores, axis=1, keepdims=True), jnp.max(own, axis=1, keepdims=True)
        )
        weights, own_weights = jnp.exp(scores - top), jnp.exp(own - top)
        total = jnp.sum(weights, axis=1, keepdims=True) + jnp.sum(
            own_weights, axis=1, keepdims=True
        )
        heads_ctx.append((weights / total).astype(jnp.bfloat16))
        heads_own.append((own_weights / total).astype(jnp.bfloat16))
    mixed_vals = product(jnp.concatenate(heads_ctx, axis=0), vals) + product(
        jnp.concatenate(heads_own, axis=0), new_kv[:, HEAD:]
    )
    attn = jnp.concatenate(
        [mixed_vals[h * half : (h + 1) * half] for h in range(QH_DEV)], axis=1
    ).astype(jnp.bfloat16)
    attn_ref[...] = attn
    out_copies[0][1].wait()
    first_ref[...] = product(attn, out_held[0]).astype(jnp.bfloat16)


def attend(resp_len, both_ctx, gains, parts, block, q_pair, cache_pair, out_pair):
    half, shard = block.shape[0], gains.shape[1]
    seqs_count, ctx_slots, width = cache_pair[0].shape
    q_width, attn_width = q_pair[0].shape[1], out_pair[0].shape[0]
    vmem = pl.BlockSpec(memory_space=pltpu.VMEM)
    smem = pl.BlockSpec(memory_space=pltpu.SMEM)
    anywhere = pl.BlockSpec(memory_space=pltpu.HBM)
    return pl.pallas_call(
        functools.partial(attention_kernel, seqs_count),
        out_shape=[
            jax.ShapeDtypeStruct((half, attn_width), jnp.bfloat16),
            jax.ShapeDtypeStruct((half, shard), jnp.bfloat16),
        ],
        in_specs=[smem] * 2 + [vmem] * 5 + [anywhere] * 6,
        out_specs=[vmem] * 2,
        scratch_shapes=[
            pltpu.VMEM((1, shard, q_width), jnp.bfloat16),
            pltpu.VMEM((2, seqs_count, ctx_slots, width), jnp.bfloat16),
            pltpu.VMEM((1, attn_width, shard), jnp.bfloat16),
            pltpu.SemaphoreType.DMA((1,)),
            pltpu.SemaphoreType.DMA((2,)),
            pltpu.SemaphoreType.DMA((1,)),
        ],
        compiler_params=pltpu.CompilerParams(vmem_limit_bytes=VMEM_LIMIT),
        name="attend",
    )(resp_len, both_ctx, gains, *parts, block, *q_pair, *cache_pair, *out_pair)


def out_kernel(attn_ref, out_own, out_other, *refs):
    outs, (held, sems) = refs[:-2], refs[-2:]
    ids = scattered_ids()
    copies = block_copies(ids[:1] + ids[2:], 1, out_own, out_other, held, sems)
    start_copies(copies)
    attn = attn_ref[...]
    for j, out in enumerate(outs):
        copies[j][1].wait()
        out[...] = product(attn, held[j]).astype(jnp.bfloat16)


def out_products(attn, out_pair):
    half, attn_width = attn.shape
    count = lax.axis_size("tensor")
    shard = out_pair[0].shape[1] * 2 // count
    vmem = pl.BlockSpec(memory_space=pltpu.VMEM)
    anywhere = pl.BlockSpec(memory_space=pltpu.HBM)
    return pl.pallas_call(
        out_kernel,
        out_shape=[jax.ShapeDtypeStruct((half, shard), jnp.bfloat16)] * (count - 1),
        in_specs=[vmem] + [anywhere] * 2,
        out_specs=[vmem] * (count - 1),
        scratch_shapes=[
            pltpu.VMEM((count - 1, attn_width, shard), jnp.bfloat16),
            pltpu.SemaphoreType.DMA((count - 1,)),
        ],
        compiler_params=pltpu.CompilerParams(vmem_limit_bytes=VMEM_LIMIT),
        cost_estimate=pl.CostEstimate(
            flops=2 * half * (count - 1) * shard * attn_width,
            bytes_accessed=2 * (count - 1) * shard * (half + attn_width),
            transcendentals=0,
        ),
        name="out_products",
    )(attn, *out_pair)


def logit_blocks(blocks, ids, copies, held, gain_ref, logits, squares):
    for j, block in enumerate(blocks):
        values = block[...]
        mixed = values.astype(jnp.float32) / gain_ref[pl.ds(ids[j], 1), :]
        squares += jnp.sum(mixed * mixed, axis=1, keepdims=True)
        copies[j][1].wait()
        logits += product(values, held[j])
    return logits, squares


def logit_kernel(gain_ref, own_ref, other_ref, *refs):
    blocks, (logits_ref, squares_ref, held, sems) = refs[:-4], refs[-4:]
    ids = gathered_ids()[: len(blocks)]
    copies = block_copies(ids, 0, own_ref, other_ref, held, sems)
    start_copies(copies)
    logits = jnp.zeros(logits_ref.shape, jnp.float32)
    squares = jnp.zeros((logits.shape[0], 1), jnp.float32)
    logits, squares = logit_blocks(blocks, ids, copies, held, gain_ref, logits, squares)
    logits_ref[...] = logits
    squares_ref[...] = jnp.broadcast_to(squares, squares_ref.shape)


def logit_part(gains, vocab_pair, blocks):
    used, (half, shard) = len(blocks), blocks[0].shape
    vocab_count = vocab_pair[0].shape[1]
    vmem = pl.BlockSpec(memory_space=pltpu.VMEM)
    anywhere = pl.BlockSpec(memory_space=pltpu.HBM)
    return pl.pallas_call(
        logit_kernel,
        out_shape=[
            jax.ShapeDtypeStruct((half, vocab_count), jnp.float32),
            jax.ShapeDtypeStruct((half, 128), jnp.float32),
        ],
        in_specs=[vmem] + [anywhere] * 2 + [vmem] * used,
        out_specs=[vmem] * 2,
        scratch_shapes=[
            pltpu.VMEM((used, shard, vocab_count), jnp.bfloat16),
            pltpu.SemaphoreType.DMA((used,)),
        ],
        compiler_params=pltpu.CompilerParams(vmem_limit_bytes=VMEM_LIMIT),
        cost_estimate=pl.CostEstimate(
            flops=2 * half * used * shard * vocab_count,
            bytes_accessed=2 * used * shard * (half + vocab_count),
            transcendentals=0,
        ),
        name="logit_part",
    )(gains, *vocab_pair, *blocks)


def stats_kernel(
    targets_ref, gain_ref, logits_ref, squares_ref, block_ref, own_ref, other_ref, stats_ref, held, sems
):
    half, shard = block_ref.shape
    ids = gathered_ids()[-1:]
    copies = block_copies(ids, 0, own_ref, other_ref, held, sems)
    start_copies(copies)
    logits, squares = logit_blocks(
        [block_ref], ids, copies, held, gain_ref, logits_ref[...], squares_ref[:, :1]
    )
    logits = logits * lax.rsqrt(squares / (shard * lax.axis_size("tensor")) + EPS)
    vocab_count = logits.shape[1]
    column_ids = lax.axis_index("tensor") * vocab_count + lax.broadcasted_iota(
        jnp.int32, (half, vocab_count), 1
    )
    picked = jnp.sum(
        jnp.where(column_ids == targets_ref[...], logits, 0.0), axis=1, keepdims=True
    )
    top = jnp.max(logits, axis=1, keepdims=True)
    total = jnp.sum(jnp.exp(logits - top), axis=1, keepdims=True)
    lane = lax.broadcasted_iota(jnp.int32, (half, 128), 1)
    stats = jnp.where(lane == 0, top, jnp.where(lane == 1, total, picked))
    stats_ref[...] = jnp.transpose(stats)[:8]


def vocab_stats(targets, gains, parts, block, vocab_pair):
    half, shard = block.shape
    vocab_count = vocab_pair[0].shape[1]
    vmem = pl.BlockSpec(memory_space=pltpu.VMEM)
    anywhere = pl.BlockSpec(memory_space=pltpu.HBM)
    return pl.pallas_call(
        stats_kernel,
        out_shape=jax.ShapeDtypeStruct((8, half), jnp.float32),
        in_specs=[vmem] * 5 + [anywhere] * 2,
        out_specs=vmem,
        scratch_shapes=[
            pltpu.VMEM((1, shard, vocab_count), jnp.bfloat16),
            pltpu.SemaphoreType.DMA((1,)),
        ],
        compiler_params=pltpu.CompilerParams(vmem_limit_bytes=VMEM_LIMIT),
        name="vocab_stats",
    )(targets.reshape(half, 1), gains, *parts, block, *vocab_pair)


def per_device(
    hidden,
    attn_gain,
    q_weight,
    kv_weight,
    kv_cache,
    out_weight,
    final_gain,
    vocab_weight,
    resp_len,
    ctx_len,
    target_ids,
):
    rows_count, shard = hidden.shape
    half = rows_count // 2
    tensor_count = lax.axis_size("tensor")
    tensor_pos = lax.axis_index("tensor")
    group = lax.axis_index("dp")
    seqs_count = kv_cache.shape[0]

    keep, send, pick = pack(resp_len, hidden, seqs_count)
    rows = keep + swap_dp(send)
    rows_f = rows.astype(jnp.float32)

    gain = lax.dynamic_slice_in_dim(attn_gain, tensor_pos * shard, shard, 0)
    kv_partial = product((rows_f * gain).astype(jnp.bfloat16), kv_weight)
    cache = kv_cache
    if kv_cache.shape[2] != 2 * HEAD:
        kv_head = tensor_pos * QH_DEV // GROUP
        cache = lax.dynamic_slice_in_dim(kv_cache, kv_head * 2 * HEAD, 2 * HEAD, 2)
    moved = {}

    def swap_rows(value):
        return lambda block: swap_dp(after(value, block))

    def swap_targets(block):
        own_targets = lax.dynamic_slice_in_dim(
            after(target_ids, block), group * rows_count, rows_count, 0
        )
        sent_targets = jnp.sum(jnp.where(pick > 0, own_targets[None, :], 0), axis=1)
        return sent_targets[:half] + swap_dp(sent_targets[None, half:])[0]

    moves = {
        "q": swap_rows(q_weight),
        "out": swap_rows(out_weight),
        "cache": swap_rows(cache),
        "ctx": lambda block: jnp.concatenate([ctx_len, swap_dp(after(ctx_len, block))], axis=0),
        "targets": swap_targets,
        "vocab": swap_rows(vocab_weight),
    }

    def moves_at(step):
        def run(block):
            for name in moves:
                if SWAP_STEP[name] == step:
                    moved[name] = moves[name](block)
            return [moved[name] for name in moves if SWAP_STEP[name] == step]

        return run

    blocks, _ = gather_blocks(
        jnp.concatenate([rows, kv_partial.astype(jnp.bfloat16)], axis=1),
        [moves_at(step) for step in range(4)],
    )
    q_other, out_other, cache_other = moved["q"], moved["out"], moved["cache"]
    both_ctx = moved["ctx"]
    q_pair, out_pair = (q_weight, q_other), (out_weight, out_other)
    gains = attn_gain.reshape(tensor_count, shard)
    parts = query_part(gains, q_pair, blocks[:-1])
    attn, first = attend(
        resp_len, both_ctx, gains, parts, blocks[-1], q_pair, (cache, cache_other), out_pair
    )
    products = out_products(attn, out_pair)
    products = [products[0], first, *products[1:]]

    partial = None
    for k in range(tensor_count // SIDE):
        total = products[2 * k].astype(jnp.float32) + swap_side(products[2 * k + 1]).astype(jnp.float32)
        if partial is not None:
            total = total + ring_step(partial).astype(jnp.float32)
        partial = total.astype(jnp.bfloat16)
    mixed = rows_f + total

    gain = lax.dynamic_slice_in_dim(final_gain, tensor_pos * shard, shard, 0)

    def place_rows(block):
        layer_rows = mixed.astype(jnp.bfloat16)
        if SWAP_STEP["layer"] > 4:
            layer_rows = after(layer_rows, block)
        layer_rows = jnp.concatenate([layer_rows, swap_dp(layer_rows)], axis=0)
        return lax.dot_general(
            pick, layer_rows, (((0,), (0,)), ((), ())), preferred_element_type=jnp.float32
        ).astype(jnp.bfloat16)

    moves["layer"] = place_rows
    blocks, _ = gather_blocks(
        (mixed * gain).astype(jnp.bfloat16), [moves_at(step) for step in range(4, 8)]
    )
    layer_out, vocab_other, targets = moved["layer"], moved["vocab"], moved["targets"]
    gains = final_gain.reshape(tensor_count, shard)
    vocab_pair = (vocab_weight, vocab_other)
    parts = logit_part(gains, vocab_pair, blocks[:-1])
    stats = vocab_stats(targets, gains, parts, blocks[-1], vocab_pair)[:3]

    def join(parts):
        top = functools.reduce(jnp.maximum, [part[0] for part in parts])
        total = sum(part[1] * jnp.exp(part[0] - top) for part in parts)
        return jnp.stack([top, total, sum(part[2] for part in parts)])

    def in_order(part, others, place):
        held = [part, *others]
        return [
            functools.reduce(
                lambda a, c: jnp.where(place(c) == p, held[c], a), range(1, len(held)), held[0]
            )
            for p in range(len(held))
        ]

    side = tensor_pos % SIDE
    corner = [
        ((1 - d) * tensor_count + (i ^ 1), d * tensor_count + i)
        for d in range(2)
        for i in range(tensor_count)
    ]
    near, far = swap_dp(stats), lax.ppermute(stats, ("dp", "tensor"), corner)
    stats = [
        join(in_order(part, [other], lambda c: side ^ c))
        for part, other in ((stats, swap_side(stats)), (near, far))
    ]
    stats = jnp.stack(stats, axis=1)
    ring_count = tensor_count // SIDE
    ring_pos = tensor_pos // SIDE
    others = [
        lax.ppermute(
            stats, "tensor", [(i, i ^ (SIDE * c)) for i in range(tensor_count)]
        )
        for c in range(1, ring_count)
    ]
    stats = join(
        in_order(stats, others, lambda c: ring_pos ^ c)
    )
    both_logprob = stats[2] - stats[0] - jnp.log(stats[1])
    token_logprob = jnp.sum(jnp.where(pick > 0, both_logprob.reshape(-1, 1), 0.0), axis=0)
    return (layer_out, token_logprob)


def solution(mesh):
    placed = (
        P(("rep", "dp"), "tensor"),
        P(),
        P("dp", "tensor"),
        P("tensor", None),
        P(("rep", "dp"), None, None),
        P("tensor", "dp"),
        P(),
        P("dp", "tensor"),
        P("rep"),
        P(("rep", "dp")),
        P("rep"),
    )
    return jax.shard_map(
        per_device,
        mesh=mesh,
        in_specs=placed,
        out_specs=(P(("rep", "dp"), "tensor"), P(("rep", "dp"))),
        check_vma=False,
    )
```

```python
import functools

import jax
import jax.numpy as jnp
from jax import lax
from jax.experimental import pallas as pl
from jax.experimental.pallas import tpu as pltpu
from jax.sharding import PartitionSpec as P

HEAD = 128
QH_DEV = 2
GROUP = 16
SIDE = 2
SWAP_STEP = {"q": 0, "out": 0, "cache": 1, "ctx": 2, "targets": 1, "layer": 5, "vocab": 5}


EPS = 1e-05
VMEM_LIMIT = 52 * 1024 * 1024


def product(left, right):
    return jnp.dot(left, right, preferred_element_type=jnp.float32)


def swap_dp(value):
    return lax.ppermute(value, "dp", [(0, 1), (1, 0)])


def swap_side(value):
    count = lax.axis_size("tensor")
    return lax.ppermute(value, "tensor", [(i, i ^ 1) for i in range(count)])


def ring_seat(seat, count):
    return jnp.where(seat == 0, 0, jnp.where(seat <= count // 2, 2 * seat - 1, 2 * (count - seat)))


def seat_of(place, count):
    return jnp.where(place % 2 == 1, (place + 1) // 2, (count - place // 2) % count)


def ring_step(value):
    count = lax.axis_size("tensor")
    ring = [0, *range(1, count // SIDE, 2), *range(count // SIDE - 2, 0, -2)]
    following = dict(zip(ring, ring[1:] + ring[:1]))
    pairs = [(i, following[i // SIDE] * SIDE + i % SIDE) for i in range(count)]
    return lax.ppermute(value, "tensor", pairs)


def after(value, *others):
    return lax.optimization_barrier((value, *others))[0]


def gather_blocks(block, beside=()):
    count = lax.axis_size("tensor") // SIDE
    blocks, values = [], []
    for k in range(count):
        crossed = swap_side(block)
        blocks += [block, crossed]
        ready = beside[k](block) if k < len(beside) else []
        values += ready
        if k + 1 < count:
            block = after(ring_step(block), crossed, *ready)
    return blocks, values


def ring_ids(first):
    count = lax.axis_size("tensor")
    pos = lax.axis_index("tensor")
    ring_count = count // SIDE
    seat = seat_of(pos // SIDE, ring_count)
    ids = []
    for k in range(first, first + ring_count):
        held = ring_seat((seat - k + 2 * ring_count) % ring_count, ring_count) * SIDE + pos % SIDE
        ids += [held, held ^ 1]
    return ids


def gathered_ids():
    return ring_ids(0)


def scattered_ids():
    return ring_ids(1)


def row_plan(lens_ref, seqs_count, half):
    group = lax.axis_index("dp")
    own = [lens_ref[group * seqs_count + i] for i in range(seqs_count)]
    other = [lens_ref[(1 - group) * seqs_count + i] for i in range(seqs_count)]
    busy = sum(own) > half
    light_total = jnp.where(busy, sum(other), sum(own))
    own_ends, busy_ends = [], []
    long_seq, long_start = jnp.int32(0), jnp.int32(0)
    own_end, busy_end = jnp.int32(0), jnp.int32(0)
    for i in range(seqs_count):
        length = jnp.where(busy, own[i], other[i])
        long_seq = jnp.where(length == half, i, long_seq)
        long_start = jnp.where(length == half, busy_end, long_start)
        own_end, busy_end = own_end + own[i], busy_end + length
        own_ends.append(own_end)
        busy_ends.append(busy_end)
    return busy, light_total, long_seq, long_start, own_ends, busy_ends


def rest_rows(slot, light_total, long_start, half):
    rest = slot - light_total
    return rest, rest + jnp.where(rest >= long_start, half, 0)


def pack_kernel(seqs_count, lens_ref, hidden_ref, keep_ref, send_ref, pick_ref):
    rows_count = hidden_ref.shape[0]
    half = rows_count // 2
    busy, light_total, _, long_start, _, _ = row_plan(lens_ref, seqs_count, half)
    slot = lax.broadcasted_iota(jnp.int32, (half, rows_count), 0)
    row = lax.broadcasted_iota(jnp.int32, (half, rows_count), 1)
    rest, rest_row = rest_rows(slot, light_total, long_start, half)
    keep_src = jnp.where(busy, long_start + slot, jnp.where(rest < 0, slot, -1))
    send_src = jnp.where(busy & (rest >= 0), rest_row, -1)
    keep_pick = jnp.where(keep_src == row, 1.0, 0.0).astype(jnp.bfloat16)
    send_pick = jnp.where(send_src == row, 1.0, 0.0).astype(jnp.bfloat16)
    pick_ref[:half] = keep_pick
    pick_ref[half:] = send_pick
    hidden = hidden_ref[...]
    send_ref[...] = product(send_pick, hidden).astype(jnp.bfloat16)
    keep_ref[...] = product(keep_pick, hidden).astype(jnp.bfloat16)


def pack(resp_len, hidden, seqs_count):
    rows_count, shard = hidden.shape
    half = rows_count // 2
    vmem = pl.BlockSpec(memory_space=pltpu.VMEM)
    return pl.pallas_call(
        functools.partial(pack_kernel, seqs_count),
        out_shape=[
            jax.ShapeDtypeStruct((half, shard), jnp.bfloat16),
            jax.ShapeDtypeStruct((half, shard), jnp.bfloat16),
            jax.ShapeDtypeStruct((rows_count, rows_count), jnp.bfloat16),
        ],
        in_specs=[pl.BlockSpec(memory_space=pltpu.SMEM), vmem],
        out_specs=[vmem] * 3,
        compiler_params=pltpu.CompilerParams(vmem_limit_bytes=VMEM_LIMIT),
        name="pack_rows",
    )(resp_len, hidden)


def block_copies(ids, axis, own_ref, other_ref, held, sems):
    count = lax.axis_size("tensor")
    group = lax.axis_index("dp")
    size = own_ref.shape[axis] * 2 // count
    copies = []
    places = held if isinstance(held, list) else [held.at[j] for j in range(len(ids))]
    for j, block in enumerate(ids):
        place = pl.ds(pl.multiple_of((block % (count // 2)) * size, size), size)
        at = (place, slice(None)) if axis == 0 else (slice(None), place)
        here = pltpu.make_async_copy(own_ref.at[at], places[j], sems.at[j])
        there = pltpu.make_async_copy(other_ref.at[at], places[j], sems.at[j])
        copies.append((block // (count // 2) == group, here, there))
    return copies


def start_copies(copies):
    for is_here, here, there in copies:
        pl.when(is_here)(here.start)
        pl.when(jnp.logical_not(is_here))(there.start)


def query_blocks(blocks, shard, ids, copies, held, gain_ref, query, new_kv, squares):
    kv_head = lax.axis_index("tensor") * QH_DEV // GROUP
    kv_place = pl.ds(pl.multiple_of(shard + kv_head * 2 * HEAD, 2 * HEAD), 2 * HEAD)
    for j, block in enumerate(blocks):
        values = block[:, :shard].astype(jnp.float32)
        squares += jnp.sum(values * values, axis=1, keepdims=True)
        gained = (values * gain_ref[pl.ds(ids[j], 1), :]).astype(jnp.bfloat16)
        new_kv += block[:, kv_place].astype(jnp.float32)
        copies[j][1].wait()
        query += product(gained, held[j])
    return query, new_kv, squares


def query_kernel(shard, gain_ref, q_own, q_other, *refs):
    blocks, (query_ref, kv_ref, squares_ref, held, sems) = refs[:-5], refs[-5:]
    ids = gathered_ids()[: len(blocks)]
    copies = block_copies(ids, 0, q_own, q_other, held, sems)
    start_copies(copies)
    query, new_kv = jnp.zeros(query_ref.shape, jnp.float32), jnp.zeros(kv_ref.shape, jnp.float32)
    squares = jnp.zeros((query.shape[0], 1), jnp.float32)
    query, new_kv, squares = query_blocks(
        blocks, shard, ids, copies, held, gain_ref, query, new_kv, squares
    )
    query_ref[...] = query
    kv_ref[...] = new_kv
    squares_ref[...] = jnp.broadcast_to(squares, squares_ref.shape)


def query_part(gains, q_pair, blocks):
    shard, used, half = gains.shape[1], len(blocks), blocks[0].shape[0]
    q_width = q_pair[0].shape[1]
    vmem = pl.BlockSpec(memory_space=pltpu.VMEM)
    anywhere = pl.BlockSpec(memory_space=pltpu.HBM)
    return pl.pallas_call(
        functools.partial(query_kernel, shard),
        out_shape=[
            jax.ShapeDtypeStruct((half, q_width), jnp.float32),
            jax.ShapeDtypeStruct((half, 2 * HEAD), jnp.float32),
            jax.ShapeDtypeStruct((half, 128), jnp.float32),
        ],
        in_specs=[vmem] + [anywhere] * 2 + [vmem] * used,
        out_specs=[vmem] * 3,
        scratch_shapes=[
            pltpu.VMEM((used, shard, q_width), jnp.bfloat16),
            pltpu.SemaphoreType.DMA((used,)),
        ],
        compiler_params=pltpu.CompilerParams(vmem_limit_bytes=VMEM_LIMIT),
        cost_estimate=pl.CostEstimate(
            flops=2 * half * used * shard * q_width,
            bytes_accessed=2 * used * shard * (half + q_width),
            transcendentals=0,
        ),
        name="query_part",
    )(gains, *q_pair, *blocks)


def attention_kernel(
    seqs_count,
    lens_ref,
    ctx_ref,
    gain_ref,
    query_ref,
    kv_ref,
    squares_ref,
    block_ref,
    q_own,
    q_other,
    cache_own,
    cache_other,
    out_own,
    out_other,
    attn_ref,
    first_ref,
    q_held,
    cache_held,
    out_held,
    q_sems,
    cache_sems,
    out_sems,
):
    half, shard = first_ref.shape
    count = lax.axis_size("tensor")
    ctx_slots = cache_own.shape[1]
    ids = gathered_ids()[-1:]
    q_copies = block_copies(ids, 0, q_own, q_other, q_held, q_sems)
    out_copies = block_copies(scattered_ids()[1:2], 1, out_own, out_other, out_held, out_sems)
    cache_copies = [
        pltpu.make_async_copy(cache_own, cache_held.at[0], cache_sems.at[0]),
        pltpu.make_async_copy(cache_other, cache_held.at[1], cache_sems.at[1]),
    ]
    start_copies(q_copies)
    for copy in cache_copies:
        copy.start()
    start_copies(out_copies)

    query, new_kv, squares = query_blocks(
        [block_ref],
        shard,
        ids,
        q_copies,
        q_held,
        gain_ref,
        query_ref[...],
        kv_ref[...],
        squares_ref[:, :1],
    )
    scale = lax.rsqrt(squares / (shard * count) + EPS)
    query = (query * scale).astype(jnp.bfloat16)
    new_kv = (new_kv * scale).astype(jnp.bfloat16)

    busy, light_total, long_seq, long_start, own_ends, busy_ends = row_plan(
        lens_ref, seqs_count, half
    )

    def segments(slot):
        rest, rest_row = rest_rows(slot, light_total, long_start, half)
        own_seg, rest_seg = jnp.zeros_like(slot), jnp.full_like(slot, seqs_count)
        for i in range(seqs_count):
            own_seg += jnp.where(slot >= own_ends[i], 1, 0)
            rest_seg += jnp.where(rest_row >= busy_ends[i], 1, 0)
        return jnp.where(busy, long_seq, jnp.where(rest < 0, own_seg, rest_seg))

    slot = lax.broadcasted_iota(jnp.int32, (half, 1), 0)
    key_slot = lax.broadcasted_iota(jnp.int32, (1, half), 1)
    seg = segments(slot)
    own_ok = (segments(key_slot) == seg) & (key_slot <= slot)
    position = lax.broadcasted_iota(jnp.int32, (half, ctx_slots), 1)

    for copy in cache_copies:
        copy.wait()
    keys = cache_held[:, :, :, :HEAD].reshape(-1, HEAD)
    vals = cache_held[:, :, :, HEAD:].reshape(-1, HEAD)
    stacked = jnp.concatenate(
        [query[:, h * HEAD : (h + 1) * HEAD] for h in range(QH_DEV)], axis=0
    )
    contract = (((1,), (1,)), ((), ()))
    ctx_scores = lax.dot_general(stacked, keys, contract, preferred_element_type=jnp.float32)
    own_scores = lax.dot_general(
        stacked, new_kv[:, :HEAD], contract, preferred_element_type=jnp.float32
    )
    ctx_scores = ctx_scores * HEAD ** (-0.5)
    own_scores = own_scores * HEAD ** (-0.5)
    heads_ctx, heads_own = [], []
    for h in range(QH_DEV):
        rows = slice(h * half, (h + 1) * half)
        pieces = []
        for i in range(2 * seqs_count):
            allowed = (seg == i) & (position < ctx_ref[i])
            piece = ctx_scores[rows, i * ctx_slots : (i + 1) * ctx_slots]
            pieces.append(jnp.where(allowed, piece, -jnp.inf))
        scores = jnp.concatenate(pieces, axis=1)
        own = jnp.where(own_ok, own_scores[rows], -jnp.inf)
        top = jnp.maximum(
            jnp.max(scores, axis=1, keepdims=True), jnp.max(own, axis=1, keepdims=True)
        )
        weights, own_weights = jnp.exp(scores - top), jnp.exp(own - top)
        total = jnp.sum(weights, axis=1, keepdims=True) + jnp.sum(
            own_weights, axis=1, keepdims=True
        )
        heads_ctx.append((weights / total).astype(jnp.bfloat16))
        heads_own.append((own_weights / total).astype(jnp.bfloat16))
    mixed_vals = product(jnp.concatenate(heads_ctx, axis=0), vals) + product(
        jnp.concatenate(heads_own, axis=0), new_kv[:, HEAD:]
    )
    attn = jnp.concatenate(
        [mixed_vals[h * half : (h + 1) * half] for h in range(QH_DEV)], axis=1
    ).astype(jnp.bfloat16)
    attn_ref[...] = attn
    out_copies[0][1].wait()
    first_ref[...] = product(attn, out_held[0]).astype(jnp.bfloat16)


def attend(resp_len, both_ctx, gains, parts, block, q_pair, cache_pair, out_pair):
    half, shard = block.shape[0], gains.shape[1]
    seqs_count, ctx_slots, width = cache_pair[0].shape
    q_width, attn_width = q_pair[0].shape[1], out_pair[0].shape[0]
    vmem = pl.BlockSpec(memory_space=pltpu.VMEM)
    smem = pl.BlockSpec(memory_space=pltpu.SMEM)
    anywhere = pl.BlockSpec(memory_space=pltpu.HBM)
    return pl.pallas_call(
        functools.partial(attention_kernel, seqs_count),
        out_shape=[
            jax.ShapeDtypeStruct((half, attn_width), jnp.bfloat16),
            jax.ShapeDtypeStruct((half, shard), jnp.bfloat16),
        ],
        in_specs=[smem] * 2 + [vmem] * 5 + [anywhere] * 6,
        out_specs=[vmem] * 2,
        scratch_shapes=[
            pltpu.VMEM((1, shard, q_width), jnp.bfloat16),
            pltpu.VMEM((2, seqs_count, ctx_slots, width), jnp.bfloat16),
            pltpu.VMEM((1, attn_width, shard), jnp.bfloat16),
            pltpu.SemaphoreType.DMA((1,)),
            pltpu.SemaphoreType.DMA((2,)),
            pltpu.SemaphoreType.DMA((1,)),
        ],
        compiler_params=pltpu.CompilerParams(vmem_limit_bytes=VMEM_LIMIT),
        name="attend",
    )(resp_len, both_ctx, gains, *parts, block, *q_pair, *cache_pair, *out_pair)


def out_kernel(attn_ref, out_own, out_other, *refs):
    outs, (held, sems) = refs[:-2], refs[-2:]
    ids = scattered_ids()
    copies = block_copies(ids[:1] + ids[2:], 1, out_own, out_other, held, sems)
    start_copies(copies)
    attn = attn_ref[...]
    for j, out in enumerate(outs):
        copies[j][1].wait()
        out[...] = product(attn, held[j]).astype(jnp.bfloat16)


def out_products(attn, out_pair):
    half, attn_width = attn.shape
    count = lax.axis_size("tensor")
    shard = out_pair[0].shape[1] * 2 // count
    vmem = pl.BlockSpec(memory_space=pltpu.VMEM)
    anywhere = pl.BlockSpec(memory_space=pltpu.HBM)
    return pl.pallas_call(
        out_kernel,
        out_shape=[jax.ShapeDtypeStruct((half, shard), jnp.bfloat16)] * (count - 1),
        in_specs=[vmem] + [anywhere] * 2,
        out_specs=[vmem] * (count - 1),
        scratch_shapes=[
            pltpu.VMEM((count - 1, attn_width, shard), jnp.bfloat16),
            pltpu.SemaphoreType.DMA((count - 1,)),
        ],
        compiler_params=pltpu.CompilerParams(vmem_limit_bytes=VMEM_LIMIT),
        cost_estimate=pl.CostEstimate(
            flops=2 * half * (count - 1) * shard * attn_width,
            bytes_accessed=2 * (count - 1) * shard * (half + attn_width),
            transcendentals=0,
        ),
        name="out_products",
    )(attn, *out_pair)


def logit_blocks(blocks, ids, copies, held, gain_ref, logits, squares):
    for j, block in enumerate(blocks):
        values = block[...]
        mixed = values.astype(jnp.float32) / gain_ref[pl.ds(ids[j], 1), :]
        squares += jnp.sum(mixed * mixed, axis=1, keepdims=True)
        copies[j][1].wait()
        logits += product(values, held[j])
    return logits, squares


def logit_kernel(gain_ref, own_ref, other_ref, *refs):
    blocks, (logits_ref, squares_ref, held, sems) = refs[:-4], refs[-4:]
    ids = gathered_ids()[: len(blocks)]
    copies = block_copies(ids, 0, own_ref, other_ref, held, sems)
    start_copies(copies)
    logits = jnp.zeros(logits_ref.shape, jnp.float32)
    squares = jnp.zeros((logits.shape[0], 1), jnp.float32)
    logits, squares = logit_blocks(blocks, ids, copies, held, gain_ref, logits, squares)
    logits_ref[...] = logits
    squares_ref[...] = jnp.broadcast_to(squares, squares_ref.shape)


def logit_part(gains, vocab_pair, blocks):
    used, (half, shard) = len(blocks), blocks[0].shape
    vocab_count = vocab_pair[0].shape[1]
    vmem = pl.BlockSpec(memory_space=pltpu.VMEM)
    anywhere = pl.BlockSpec(memory_space=pltpu.HBM)
    return pl.pallas_call(
        logit_kernel,
        out_shape=[
            jax.ShapeDtypeStruct((half, vocab_count), jnp.float32),
            jax.ShapeDtypeStruct((half, 128), jnp.float32),
        ],
        in_specs=[vmem] + [anywhere] * 2 + [vmem] * used,
        out_specs=[vmem] * 2,
        scratch_shapes=[
            pltpu.VMEM((used, shard, vocab_count), jnp.bfloat16),
            pltpu.SemaphoreType.DMA((used,)),
        ],
        compiler_params=pltpu.CompilerParams(vmem_limit_bytes=VMEM_LIMIT),
        cost_estimate=pl.CostEstimate(
            flops=2 * half * used * shard * vocab_count,
            bytes_accessed=2 * used * shard * (half + vocab_count),
            transcendentals=0,
        ),
        name="logit_part",
    )(gains, *vocab_pair, *blocks)


def stats_kernel(
    targets_ref, gain_ref, logits_ref, squares_ref, block_ref, own_ref, other_ref, stats_ref, held, sems
):
    half, shard = block_ref.shape
    ids = gathered_ids()[-1:]
    copies = block_copies(ids, 0, own_ref, other_ref, held, sems)
    start_copies(copies)
    logits, squares = logit_blocks(
        [block_ref], ids, copies, held, gain_ref, logits_ref[...], squares_ref[:, :1]
    )
    logits = logits * lax.rsqrt(squares / (shard * lax.axis_size("tensor")) + EPS)
    vocab_count = logits.shape[1]
    column_ids = lax.axis_index("tensor") * vocab_count + lax.broadcasted_iota(
        jnp.int32, (half, vocab_count), 1
    )
    picked = jnp.sum(
        jnp.where(column_ids == targets_ref[...], logits, 0.0), axis=1, keepdims=True
    )
    top = jnp.max(logits, axis=1, keepdims=True)
    total = jnp.sum(jnp.exp(logits - top), axis=1, keepdims=True)
    lane = lax.broadcasted_iota(jnp.int32, (half, 128), 1)
    stats = jnp.where(lane == 0, top, jnp.where(lane == 1, total, picked))
    stats_ref[...] = jnp.transpose(stats)[:8]


def vocab_stats(targets, gains, parts, block, vocab_pair):
    half, shard = block.shape
    vocab_count = vocab_pair[0].shape[1]
    vmem = pl.BlockSpec(memory_space=pltpu.VMEM)
    anywhere = pl.BlockSpec(memory_space=pltpu.HBM)
    return pl.pallas_call(
        stats_kernel,
        out_shape=jax.ShapeDtypeStruct((8, half), jnp.float32),
        in_specs=[vmem] * 5 + [anywhere] * 2,
        out_specs=vmem,
        scratch_shapes=[
            pltpu.VMEM((1, shard, vocab_count), jnp.bfloat16),
            pltpu.SemaphoreType.DMA((1,)),
        ],
        compiler_params=pltpu.CompilerParams(vmem_limit_bytes=VMEM_LIMIT),
        name="vocab_stats",
    )(targets.reshape(half, 1), gains, *parts, block, *vocab_pair)


def per_device(
    hidden,
    attn_gain,
    q_weight,
    kv_weight,
    kv_cache,
    out_weight,
    final_gain,
    vocab_weight,
    resp_len,
    ctx_len,
    target_ids,
):
    rows_count, shard = hidden.shape
    half = rows_count // 2
    tensor_count = lax.axis_size("tensor")
    tensor_pos = lax.axis_index("tensor")
    group = lax.axis_index("dp")
    seqs_count = kv_cache.shape[0]

    keep, send, pick = pack(resp_len, hidden, seqs_count)
    rows = keep + swap_dp(send)
    rows_f = rows.astype(jnp.float32)

    gain = lax.dynamic_slice_in_dim(attn_gain, tensor_pos * shard, shard, 0)
    kv_partial = product((rows_f * gain).astype(jnp.bfloat16), kv_weight)
    cache = kv_cache
    if kv_cache.shape[2] != 2 * HEAD:
        kv_head = tensor_pos * QH_DEV // GROUP
        cache = lax.dynamic_slice_in_dim(kv_cache, kv_head * 2 * HEAD, 2 * HEAD, 2)
    moved = {}

    def swap_rows(value):
        return lambda block: swap_dp(after(value, block))

    def swap_targets(block):
        own_targets = lax.dynamic_slice_in_dim(
            after(target_ids, block), group * rows_count, rows_count, 0
        )
        sent_targets = jnp.sum(jnp.where(pick > 0, own_targets[None, :], 0), axis=1)
        return sent_targets[:half] + swap_dp(sent_targets[None, half:])[0]

    moves = {
        "q": swap_rows(q_weight),
        "out": swap_rows(out_weight),
        "cache": swap_rows(cache),
        "ctx": lambda block: jnp.concatenate([ctx_len, swap_dp(after(ctx_len, block))], axis=0),
        "targets": swap_targets,
        "vocab": swap_rows(vocab_weight),
    }

    def moves_at(step):
        def run(block):
            for name in moves:
                if SWAP_STEP[name] == step:
                    moved[name] = moves[name](block)
            return [moved[name] for name in moves if SWAP_STEP[name] == step]

        return run

    blocks, _ = gather_blocks(
        jnp.concatenate([rows, kv_partial.astype(jnp.bfloat16)], axis=1),
        [moves_at(step) for step in range(4)],
    )
    q_other, out_other, cache_other = moved["q"], moved["out"], moved["cache"]
    both_ctx = moved["ctx"]
    q_pair, out_pair = (q_weight, q_other), (out_weight, out_other)
    gains = attn_gain.reshape(tensor_count, shard)
    parts = query_part(gains, q_pair, blocks[:-1])
    attn, first = attend(
        resp_len, both_ctx, gains, parts, blocks[-1], q_pair, (cache, cache_other), out_pair
    )
    products = out_products(attn, out_pair)
    products = [products[0], first, *products[1:]]

    partial = None
    for k in range(tensor_count // SIDE):
        total = products[2 * k].astype(jnp.float32) + swap_side(products[2 * k + 1]).astype(jnp.float32)
        if partial is not None:
            total = total + ring_step(partial).astype(jnp.float32)
        partial = total.astype(jnp.bfloat16)
    mixed = rows_f + total

    gain = lax.dynamic_slice_in_dim(final_gain, tensor_pos * shard, shard, 0)

    def place_rows(block):
        layer_rows = mixed.astype(jnp.bfloat16)
        if SWAP_STEP["layer"] > 4:
            layer_rows = after(layer_rows, block)
        layer_rows = jnp.concatenate([layer_rows, swap_dp(layer_rows)], axis=0)
        return lax.dot_general(
            pick, layer_rows, (((0,), (0,)), ((), ())), preferred_element_type=jnp.float32
        ).astype(jnp.bfloat16)

    moves["layer"] = place_rows
    blocks, _ = gather_blocks(
        (mixed * gain).astype(jnp.bfloat16), [moves_at(step) for step in range(4, 8)]
    )
    layer_out, vocab_other, targets = moved["layer"], moved["vocab"], moved["targets"]
    gains = final_gain.reshape(tensor_count, shard)
    vocab_pair = (vocab_weight, vocab_other)
    parts = logit_part(gains, vocab_pair, blocks[:-1])
    stats = vocab_stats(targets, gains, parts, blocks[-1], vocab_pair)[:3]

    def join(parts):
        top = functools.reduce(jnp.maximum, [part[0] for part in parts])
        total = sum(part[1] * jnp.exp(part[0] - top) for part in parts)
        return jnp.stack([top, total, sum(part[2] for part in parts)])

    def in_order(part, others, place):
        held = [part, *others]
        return [
            functools.reduce(
                lambda a, c: jnp.where(place(c) == p, held[c], a), range(1, len(held)), held[0]
            )
            for p in range(len(held))
        ]

    side = tensor_pos % SIDE
    corner = [
        ((1 - d) * tensor_count + (i ^ 1), d * tensor_count + i)
        for d in range(2)
        for i in range(tensor_count)
    ]
    near, far = swap_dp(stats), lax.ppermute(stats, ("dp", "tensor"), corner)
    stats = [
        join(in_order(part, [other], lambda c: side ^ c))
        for part, other in ((stats, swap_side(stats)), (near, far))
    ]
    stats = jnp.stack(stats, axis=1)
    ring_count = tensor_count // SIDE
    ring_pos = tensor_pos // SIDE
    others = [
        lax.ppermute(
            stats, "tensor", [(i, i ^ (SIDE * c)) for i in range(tensor_count)]
        )
        for c in range(1, ring_count)
    ]
    stats = join(
        in_order(stats, others, lambda c: ring_pos ^ c)
    )
    both_logprob = stats[2] - stats[0] - jnp.log(stats[1])
    token_logprob = jnp.sum(jnp.where(pick > 0, both_logprob.reshape(-1, 1), 0.0), axis=0)
    return (layer_out, token_logprob)


def solution(mesh):
    placed = (
        P(("rep", "dp"), "tensor"),
        P(),
        P("dp", "tensor"),
        P("tensor", None),
        P(("rep", "dp"), None, None),
        P("tensor", "dp"),
        P(),
        P("dp", "tensor"),
        P("rep"),
        P(("rep", "dp")),
        P("rep"),
    )
    return jax.shard_map(
        per_device,
        mesh=mesh,
        in_specs=placed,
        out_specs=(P(("rep", "dp"), "tensor"), P(("rep", "dp"))),
        check_vma=False,
    )
```
